256 devices in a mesh: seq: 64 (over y, x, z_hi, core), head: 4 (over z_lo).
Axes of the slice: x: 4, y: 4, z: 8 (z_hi: 2, z_lo: 4; z = z_hi * 4 + z_lo), core: 2. Of those that a mesh axis runs over, the one named last changes fastest.
Arguments:
- query_rows: bfloat16 [16384, 5120], P('seq', 'head'), may hold values from -6 to 6
- key_rows: bfloat16 [16384, 5120], P('seq', 'head'), may hold values from -6 to 6
- value_rows: bfloat16 [16384, 5120], P('seq', 'head'), may hold values from -6 to 6
- attn_out: bfloat16 [16384, 5120], P('seq', 'head'), may hold values from -3 to 3
- log_total: float32 [40, 16384], P('head', 'seq'), as said below
- d_layer: bfloat16 [16384, 5120], P('seq', 'head'), may hold values from -6 to 6
- w_output: bfloat16 [5120, 5120], P('seq', 'head'), may hold values from -0.078125 to 0.078125
Outputs:
- d_query: bfloat16 [16384, 5120], P('seq', 'head')
- d_key: bfloat16 [16384, 5120], P('seq', 'head')
- d_value: bfloat16 [16384, 5120], P('seq', 'head')
The draws below stay inside these ranges and needn't reach their ends.
Inputs may be any that keep to these rules, and one draw needn't show every extreme that they name: log_total[h, i] is the log of the sum of exp(score) over the keys allowed for row i of head h.
All inputs are finite; a program needn't handle non-finite values.
Results may differ from the reference program's by a relative error of at most 0.009.
Values may be sent and summed in bfloat16 or wider, within the bound.
A program may use at most 64 MiB of HBM per device.

```python
import jax
import jax.numpy as jnp
from jax import lax

D = 5120
HD = 128
TOK_DEV = 256
HEADS = 40
TOKENS = 16384


def shared_rows(key):
    shape = (TOKENS, HEADS * HD)
    normal_query = jnp.clip(1.4 * jax.random.normal(jax.random.fold_in(key, 21), shape, jnp.float32), -6.0, 6.0)
    normal_keys = jnp.clip(1.4 * jax.random.normal(jax.random.fold_in(key, 23), shape, jnp.float32), -6.0, 6.0)
    query = normal_query.astype(jnp.bfloat16)
    keys = normal_keys.astype(jnp.bfloat16)
    return (query, keys)


def draw_query_rows(key, part):
    rows = shared_rows(key)
    return rows[0]


def draw_key_rows(key, part):
    rows = shared_rows(key)
    return rows[1]


def draw_log_total(key, part):
    rows = shared_rows(key)
    query = rows[0].astype(jnp.float32)
    keys = rows[1].astype(jnp.float32)
    blocks = TOKENS // TOK_DEV
    padding = jnp.zeros((TOK_DEV, HEADS * HD), jnp.float32)
    key_pad = jnp.concatenate([padding, keys], axis=0)
    offsets = jnp.arange(TOK_DEV, dtype=jnp.int32)
    span = jnp.arange(2 * TOK_DEV, dtype=jnp.int32)

    def block_stats(block):
        start = (block * TOK_DEV).astype(jnp.int32)
        query_blk = lax.dynamic_slice_in_dim(query, start, TOK_DEV, 0).reshape(TOK_DEV, HEADS, HD)
        key_win = lax.dynamic_slice_in_dim(key_pad, start, 2 * TOK_DEV, 0).reshape(2 * TOK_DEV, HEADS, HD)
        raw_scores = jnp.einsum('qhd,khd->hqk', query_blk, key_win, precision=lax.Precision.HIGHEST) * HD ** (-0.5)
        query_pos = block * TOK_DEV + offsets
        key_pos = (block - 1) * TOK_DEV + span
        allowed = ((key_pos[None, :] <= query_pos[:, None]) & (key_pos[None, :] >= 0))[None]
        masked = jnp.where(allowed, raw_scores, -1e+30)
        row_top = jnp.max(masked, axis=2)
        row_total = jnp.sum(jnp.where(allowed, jnp.exp(masked - row_top[:, :, None]), 0.0), axis=2)
        return row_top + jnp.log(row_total)
    stats = lax.map(block_stats, jnp.arange(blocks, dtype=jnp.int32))
    return stats.transpose(1, 0, 2).reshape(HEADS, TOKENS).astype(jnp.float32)


def block_levels(own_key, extent, split, smallest, top_value):
    def one(position, parts):
        draws = jax.random.uniform(jax.random.fold_in(jax.random.fold_in(own_key, 6), position), (parts,), jnp.float32, smallest / len(split), top_value / len(split))
        return jnp.repeat(jnp.exp(draws), extent[position] // parts).reshape((-1,) + (1,) * (len(extent) - position - 1))

    factor_of = one(*split[0])
    for cut in split[1:]:
        factor_of = factor_of * one(*cut)
    return factor_of


def bell_draw(rng, extent, deviation, reach, shards=(), kind=jnp.bfloat16):
    values = jax.random.normal(rng, extent, jnp.float32) * deviation
    if len(shards) > 0:
        values = block_levels(rng, extent, shards, -0.22, 0.18) * values
    return jnp.clip(values, min=-reach, max=reach).astype(kind)


def setup_inputs(seed: int = 0) -> dict:
    key_of = jax.random.split(jax.random.key(seed), 8)
    return {
        "query_rows": draw_query_rows(jax.random.fold_in(key_of[7], 71), 0),
        "key_rows": draw_key_rows(jax.random.fold_in(key_of[7], 71), 0),
        "value_rows": bell_draw(key_of[2], (TOKENS, HEADS * HD), 1.0, 6.0, ((0, 64), (1, 4))),
        "attn_out": bell_draw(key_of[3], (TOKENS, HEADS * HD), 0.5, 3.0, ((0, 64), (1, 4))),
        "log_total": draw_log_total(jax.random.fold_in(key_of[7], 71), 0),
        "d_layer": bell_draw(key_of[5], (TOKENS, D), 1.0, 6.0, ((0, 64), (1, 4))),
        "w_output": bell_draw(key_of[6], (HEADS * HD, D), D ** -0.5, 0.078125, ((0, 64), (1, 4))),
    }


big_negative = -1.0e30


def reference(query_rows, key_rows, value_rows, attn_out, log_total, d_layer, w_output):
    score_scale = HD ** -0.5
    highest = lax.Precision.HIGHEST
    col_count = HEADS * HD
    d_attn = jnp.dot(d_layer, w_output.T, preferred_element_type=jnp.float32).astype(jnp.bfloat16)
    blocks = TOKENS // TOK_DEV

    def split_heads(array):
        return array.astype(jnp.float32).reshape(blocks, TOK_DEV, HEADS, HD)

    query_all = split_heads(query_rows)
    dout_all = split_heads(d_attn)
    row_delta = jnp.sum(dout_all * split_heads(attn_out), axis=3).transpose(0, 2, 1)
    log_blocks = log_total.reshape(HEADS, blocks, TOK_DEV).transpose(1, 0, 2)
    padding = jnp.zeros((TOK_DEV, col_count), jnp.float32)
    key_pad = jnp.concatenate([padding, key_rows.astype(jnp.float32)], axis=0)
    value_pad = jnp.concatenate([padding, value_rows.astype(jnp.float32)], axis=0)
    offsets = jnp.arange(TOK_DEV, dtype=jnp.int32)
    span = jnp.arange(2 * TOK_DEV, dtype=jnp.int32)

    def block_pass(block):
        query_blk = query_all[block]
        dout_blk = dout_all[block]
        log_blk = log_blocks[block]
        delta_blk = row_delta[block]
        start = (block * TOK_DEV).astype(jnp.int32)
        key_win = lax.dynamic_slice_in_dim(key_pad, start, 2 * TOK_DEV, 0).reshape(2 * TOK_DEV, HEADS, HD)
        value_win = lax.dynamic_slice_in_dim(value_pad, start, 2 * TOK_DEV, 0).reshape(2 * TOK_DEV, HEADS, HD)
        query_pos = block * TOK_DEV + offsets
        key_pos = (block - 1) * TOK_DEV + span
        allowed = (key_pos[None, :] <= query_pos[:, None]) & (key_pos[None, :] >= 0)
        raw_scores = jnp.einsum("qhd,khd->hqk", query_blk, key_win, precision=highest) * score_scale
        probs_full = jnp.exp(jnp.where(allowed[None], raw_scores, big_negative) - log_blk[:, :, None])
        probs_low = lax.optimization_barrier(probs_full.astype(jnp.bfloat16)).astype(jnp.float32)
        grad_value = jnp.einsum("hqk,qhd->khd", probs_low, dout_blk, precision=highest)
        grad_probs = jnp.einsum("qhd,khd->hqk", dout_blk, value_win, precision=highest)
        grad_scores = probs_full * (grad_probs - delta_blk[:, :, None])
        scores_low = lax.optimization_barrier(grad_scores.astype(jnp.bfloat16)).astype(jnp.float32)
        grad_query = jnp.einsum("hqk,khd->qhd", scores_low, key_win, precision=highest) * score_scale
        grad_key = jnp.einsum("hqk,qhd->khd", scores_low, query_blk, precision=highest) * score_scale
        return (grad_query.reshape(TOK_DEV, col_count), grad_key.reshape(2 * TOK_DEV, col_count), grad_value.reshape(2 * TOK_DEV, col_count))

    grad_query, grad_key, grad_value = lax.map(block_pass, jnp.arange(blocks, dtype=jnp.int32))
    tail = jnp.zeros((1, TOK_DEV, col_count), jnp.float32)
    key_total = grad_key[:, TOK_DEV:] + jnp.concatenate([grad_key[1:, :TOK_DEV], tail], axis=0)
    value_total = grad_value[:, TOK_DEV:] + jnp.concatenate([grad_value[1:, :TOK_DEV], tail], axis=0)
    d_query = grad_query.reshape(TOKENS, col_count).astype(jnp.bfloat16)
    d_key = key_total.reshape(TOKENS, col_count).astype(jnp.bfloat16)
    d_value = value_total.reshape(TOKENS, col_count).astype(jnp.bfloat16)
    return d_query, d_key, d_value
```

```python
import functools

import jax
import jax.numpy as jnp
from jax import lax
from jax.experimental import pallas as pl
from jax.experimental.pallas import tpu as pltpu
from jax.sharding import PartitionSpec as P

HD = 128
SCALE = HD ** (-0.5)
MASKED = -1e30
CHUNK = 256
MESH = pl.DeviceIdType.MESH
NT = (((1,), (1,)), ((), ()))
NN = (((1,), (0,)), ((), ()))
TN = (((0,), (0,)), ((), ()))


def dot(a, b, dims):
    return lax.dot_general(a, b, dims, preferred_element_type=jnp.float32)


def kernel(
    q_hbm, k_hbm, v_hbm, ao_hbm, log_hbm, dl_hbm, w_hbm,
    dq_ref, dk_ref, dv_ref,
    wbuf, dl, q, k, v, ao, logs, q_next, log_next,
    keep, send1, recv1, send2, recv2, do, do_next, delta, delta_next,
    dq_acc, dk_acc, dv_acc, dq_send, dq_recv,
    local_sem, w_send, w_recv, one_send, one_recv, two_send, two_recv,
    q_send, q_rsem, do_send, do_rsem, delta_send, delta_rsem, back_send, back_rsem,
):
    seq = lax.axis_index("seq")
    zlo = lax.axis_index("head")
    core = lax.rem(seq, 2)
    zhi = lax.rem(seq // 2, 2)
    x = lax.rem(seq // 4, 4)
    y = seq // 16
    shard = w_hbm.shape[0]
    chunks = q.shape[1] // CHUNK
    heads = CHUNK // HD

    def slot(yy, xx, hh, cc):
        return ((lax.rem(yy + 4, 4) * 4 + lax.rem(xx + 4, 4)) * 2 + hh) * 2 + cc

    sibling = (slot(y, x, zhi, 1 - core), zlo)
    far = (slot(y, x, 1 - zhi, core), zlo)
    before = (lax.rem(seq + 63, 64), zlo)
    after = (lax.rem(seq + 1, 64), zlo)
    flip1 = zlo + 1 - 2 * lax.rem(zlo, 2)
    flip2 = lax.rem(zlo + 2, 4)
    side1 = (seq, flip1)
    side2 = (seq, flip2)

    def at(f, i, j):
        return slot(y + f * i + (1 - f) * j, x + (1 - f) * i + f * j, f, core)

    def near(f, i, j):
        return (slot(y + f * i + (1 - f) * j, x + (1 - f) * i + f * j, zhi, core), zlo)

    loads = [
        pltpu.make_async_copy(src, dst, local_sem.at[n])
        for n, (src, dst) in enumerate(
            [(dl_hbm, dl), (q_hbm, q), (k_hbm, k), (v_hbm, v), (ao_hbm, ao), (log_hbm, logs)]
        )
    ]

    def w_rows(s):
        return wbuf.at[pl.ds(pl.multiple_of(s * shard, 16), shard)]

    own = pltpu.make_async_copy(w_hbm, w_rows(seq), w_recv.at[seq])
    own.start()
    for c in loads:
        c.start()

    barrier = pltpu.get_barrier_semaphore()
    partners = [sibling, far, before, after, side1, side2]
    for d in (1, -1):
        partners += [near(0, d, 0), near(0, 0, d)]
    for p in partners:
        pl.semaphore_signal(barrier, inc=1, device_id=p, device_id_type=MESH)
    pl.semaphore_wait(barrier, len(partners))

    w_sends = []

    def w_copy(s, device, n):
        return pltpu.make_async_remote_copy(
            w_rows(s), w_rows(s), w_send.at[n], w_recv.at[s],
            device_id=device, device_id_type=MESH,
        )

    def send_w(s, device):
        c = w_copy(s, device, len(w_sends))
        c.start()
        w_sends.append(c)

    def wait_w(s):
        w_copy(s, sibling, 0).wait_recv()

    own.wait()
    send_w(seq, far)
    zf, zg = zhi, 1 - zhi

    def begin(f):
        s = at(f, 0, 0)
        for d in (1, -1):
            send_w(s, near(f, d, 0))
            send_w(s, near(f, 0, d))
        send_w(s, sibling)

    def spread(f, i):
        s = at(f, i, 0)
        for d in (1, -1):
            send_w(s, near(f, 0, d))
        send_w(s, sibling)

    def first_near(f):
        wait_w(at(f, 1, 0))
        wait_w(at(f, -1, 0))
        step = 1 - 2 * core
        send_w(at(f, -step, 0), near(f, step, 0))
        spread(f, 1)
        spread(f, -1)

    def first_far(f):
        wait_w(at(f, 2, 0))
        spread(f, 2)

    def second_near(f, i):
        for d in (1, -1):
            wait_w(at(f, i, d))
        d = 1 if i in (0, 1) else -1
        send_w(at(f, i, -d), near(f, 0, d))
        for d in (1, -1):
            send_w(at(f, i, d), sibling)

    def second_far(f, i):
        wait_w(at(f, i, 2))
        send_w(at(f, i, 2), sibling)

    def cross_wait(h):
        for xx in range(4):
            for hh in range(2):
                wait_w(slot(h, xx, hh, 1 - core))

    def one_copy(j, t):
        return pltpu.make_async_remote_copy(
            send1.at[j, t], recv1.at[j, t], one_send.at[j, t], one_recv.at[j, t],
            device_id=side1, device_id_type=MESH,
        )

    def two_copy(t):
        return pltpu.make_async_remote_copy(
            send2.at[t], recv2.at[t], two_send.at[t], two_recv.at[t],
            device_id=side2, device_id_type=MESH,
        )

    def group(d):
        h = lax.rem(y + d + 4, 4)
        cross_wait(h)
        mine = lax.rem(h + zlo, 2) == 0

        def product(t):
            rows = pl.ds(pl.multiple_of(h * (chunks * CHUNK) + t * CHUNK, CHUNK), CHUNK)
            return dot(dl[...], wbuf[rows, :], NT)

        @pl.when(mine)
        def _():
            j = jnp.where(h == zlo, 0, 1)

            def body(t, carry):
                keep[j, t] = product(t)
                return carry

            lax.fori_loop(0, chunks, body, 0)

        @pl.when(jnp.logical_not(mine))
        def _():
            j = jnp.where(h == flip1, 0, 1)

            def body(t, carry):
                send1[j, t] = product(t).astype(jnp.bfloat16)
                one_copy(j, t).start()
                return carry

            lax.fori_loop(0, chunks, body, 0)

    begin(zf)
    first_near(zf)
    wait_w(at(zg, 0, 0))
    begin(zg)
    q_copy = pltpu.make_async_remote_copy(
        q, q_next, q_send.at[0], q_rsem.at[0], device_id=before, device_id_type=MESH
    )
    log_copy = pltpu.make_async_remote_copy(
        logs, log_next, q_send.at[1], q_rsem.at[1], device_id=before, device_id_type=MESH
    )
    for c in loads:
        c.wait()
    q_copy.start()
    log_copy.start()
    first_far(zf)
    first_near(zg)
    second_near(zf, 0)
    first_far(zg)
    second_near(zf, 1)
    second_near(zg, 0)
    second_near(zf, -1)
    second_near(zg, 1)
    second_near(zf, 2)
    second_near(zg, -1)
    second_far(zf, 0)
    second_far(zg, 0)
    group(0)
    second_near(zg, 2)
    second_far(zf, 1)
    second_far(zg, 1)
    group(1)
    second_far(zf, -1)
    second_far(zg, -1)
    group(-1)
    second_far(zf, 2)
    second_far(zg, 2)
    group(2)

    def combine(t, carry):
        one_copy(1, t).wait_recv()
        send2[t] = (keep[1, t] + recv1[1, t].astype(jnp.float32)).astype(jnp.bfloat16)
        two_copy(t).start()
        return carry

    lax.fori_loop(0, chunks, combine, 0)

    def do_copy(t):
        return pltpu.make_async_remote_copy(
            do.at[t], do_next.at[t], do_send.at[t], do_rsem.at[t],
            device_id=before, device_id_type=MESH,
        )

    def delta_copy(t):
        return pltpu.make_async_remote_copy(
            delta.at[t], delta_next.at[t], delta_send.at[t], delta_rsem.at[t],
            device_id=before, device_id_type=MESH,
        )

    def back_copy(t):
        return pltpu.make_async_remote_copy(
            dq_send.at[t], dq_recv.at[t], back_send.at[t], back_rsem.at[t],
            device_id=after, device_id_type=MESH,
        )

    def cols(t, n):
        return pl.ds(pl.multiple_of(t * CHUNK + n * HD, HD), HD)

    def finish(t, carry):
        one_copy(0, t).wait_recv()
        two_copy(t).wait_recv()
        total = keep[0, t] + recv1[0, t].astype(jnp.float32) + recv2[t].astype(jnp.float32)
        do[t] = total.astype(jnp.bfloat16)
        do_copy(t).start()
        for n in range(heads):
            prod = do[t, :, n * HD:(n + 1) * HD].astype(jnp.float32) * ao[:, cols(t, n)].astype(jnp.float32)
            row = jnp.sum(prod.T, axis=0, keepdims=True)
            delta[t, n * 8:(n + 1) * 8, :] = jnp.broadcast_to(row, (8, row.shape[1]))
        delta_copy(t).start()
        return carry

    lax.fori_loop(0, chunks, finish, 0)

    rows_i = q.shape[0]
    key_at = lax.broadcasted_iota(jnp.int32, (rows_i, rows_i), 0)
    query_at = lax.broadcasted_iota(jnp.int32, (rows_i, rows_i), 1)

    def head_grads(qh, kh, vh, doh, log_row, delta_row, allowed):
        score = dot(kh, qh, NT) * SCALE - log_row
        probs = jnp.exp(jnp.where(allowed, score, MASKED))
        g_value = dot(probs.astype(jnp.bfloat16), doh, NN)
        g_probs = dot(vh, doh, NT)
        low = (probs * (g_probs - delta_row)).astype(jnp.bfloat16)
        g_key = dot(low, qh, NN) * SCALE
        g_query = dot(low, kh, TN) * SCALE
        return g_query, g_key, g_value

    def diagonal(t, carry):
        for n in range(heads):
            c = cols(t, n)
            part = slice(n * HD, (n + 1) * HD)
            g = head_grads(
                q[:, c], k[:, c], v[:, c], do[t, :, part],
                logs[pl.ds(t * heads + n, 1), :], delta[t, n * 8:n * 8 + 1, :],
                key_at <= query_at,
            )
            dq_acc[t, :, part], dk_acc[t, :, part], dv_acc[t, :, part] = g
        return carry

    lax.fori_loop(0, chunks, diagonal, 0)

    q_copy.wait_recv()
    log_copy.wait_recv()
    limit = jnp.where(seq < 63, rows_i, 0)

    def crossing(t, carry):
        do_copy(t).wait_recv()
        delta_copy(t).wait_recv()
        for n in range(heads):
            c = cols(t, n)
            part = slice(n * HD, (n + 1) * HD)
            g_query, g_key, g_value = head_grads(
                q_next[:, c], k[:, c], v[:, c], do_next[t, :, part],
                log_next[pl.ds(t * heads + n, 1), :], delta_next[t, n * 8:n * 8 + 1, :],
                key_at < limit,
            )
            dq_send[t, :, part] = g_query.astype(jnp.bfloat16)
            dk_ref[:, c] = (dk_acc[t, :, part] + g_key).astype(jnp.bfloat16)
            dv_ref[:, c] = (dv_acc[t, :, part] + g_value).astype(jnp.bfloat16)
        back_copy(t).start()
        return carry

    lax.fori_loop(0, chunks, crossing, 0)

    def close(t, carry):
        back_copy(t).wait_recv()
        c = pl.ds(pl.multiple_of(t * CHUNK, CHUNK), CHUNK)
        dq_ref[:, c] = (dq_acc[t] + dq_recv[t].astype(jnp.float32)).astype(jnp.bfloat16)
        return carry

    lax.fori_loop(0, chunks, close, 0)

    for c in w_sends:
        c.wait_send()
    q_copy.wait_send()
    log_copy.wait_send()

    def drain(t, carry):
        one_copy(0, t).wait_send()
        one_copy(1, t).wait_send()
        two_copy(t).wait_send()
        do_copy(t).wait_send()
        delta_copy(t).wait_send()
        back_copy(t).wait_send()
        return carry

    lax.fori_loop(0, chunks, drain, 0)


def on_device(query_rows, key_rows, value_rows, attn_out, log_total, d_layer, w_output):
    rows, width = query_rows.shape
    n_heads = log_total.shape[0]
    chunks = width // CHUNK
    seqs = lax.axis_size("seq")
    bf, f32 = jnp.bfloat16, jnp.float32
    full = (rows, width)
    cut = (chunks, rows, CHUNK)
    dma = pltpu.SemaphoreType.DMA
    vm = pltpu.VMEM
    scratch = [
        vm((w_output.shape[0] * seqs, width), bf),
        vm(full, bf), vm(full, bf), vm(full, bf), vm(full, bf), vm(full, bf),
        vm((n_heads, rows), f32), vm(full, bf), vm((n_heads, rows), f32),
        vm((2,) + cut, f32), vm((2,) + cut, bf), vm((2,) + cut, bf),
        vm(cut, bf), vm(cut, bf), vm(cut, bf), vm(cut, bf),
        vm((chunks, 16, rows), f32), vm((chunks, 16, rows), f32),
        vm(cut, f32), vm(cut, f32), vm(cut, f32), vm(cut, bf), vm(cut, bf),
        dma((6,)), dma((64,)), dma((64,)), dma((2, chunks)), dma((2, chunks)),
        dma((chunks,)), dma((chunks,)), dma((2,)), dma((2,)),
        dma((chunks,)), dma((chunks,)), dma((chunks,)), dma((chunks,)),
        dma((chunks,)), dma((chunks,)),
    ]
    out = jax.ShapeDtypeStruct(full, bf)
    return pl.pallas_call(
        kernel,
        out_shape=(out, out, out),
        in_specs=[pl.BlockSpec(memory_space=pl.ANY)] * 7,
        out_specs=[pl.BlockSpec(memory_space=pltpu.VMEM)] * 3,
        scratch_shapes=scratch,
        compiler_params=pltpu.CompilerParams(
            collective_id=0, has_side_effects=True, vmem_limit_bytes=56 * 2**20
        ),
    )(query_rows, key_rows, value_rows, attn_out, log_total, d_layer, w_output)


def solution(mesh):
    spec = P("seq", "head")
    return jax.shard_map(
        on_device,
        mesh=mesh,
        in_specs=(spec, spec, spec, spec, P("head", "seq"), spec, spec),
        out_specs=(spec, spec, spec),
        check_vma=False,
    )
```

```python
import functools

import jax
import jax.numpy as jnp
from jax import lax
from jax.experimental import pallas as pl
from jax.experimental.pallas import tpu as pltpu
from jax.sharding import PartitionSpec as P

HD = 128
SCALE = HD ** (-0.5)
MASKED = -1e30
CHUNK = 256
MESH = pl.DeviceIdType.MESH
NT = (((1,), (1,)), ((), ()))
NN = (((1,), (0,)), ((), ()))
TN = (((0,), (0,)), ((), ()))


def dot(a, b, dims):
    return lax.dot_general(a, b, dims, preferred_element_type=jnp.float32)


def kernel(
    q_hbm, k_hbm, v_hbm, ao_hbm, log_hbm, dl_hbm, w_hbm,
    dq_ref, dk_ref, dv_ref,
    wbuf, dl, q, k, v, ao, ao_t, logs, q_next, log_next,
    keep, send1, recv1, send2, recv2, do, do_next, delta, delta_next,
    dq_acc, dk_acc, dv_acc, dq_send, dq_recv,
    local_sem, w_send, w_recv, one_send, one_recv, two_send, two_recv,
    q_send, q_rsem, do_send, do_rsem, delta_send, delta_rsem, back_send, back_rsem,
):
    seq = lax.axis_index("seq")
    zlo = lax.axis_index("head")
    core = lax.rem(seq, 2)
    zhi = lax.rem(seq // 2, 2)
    x = lax.rem(seq // 4, 4)
    y = seq // 16
    shard = w_hbm.shape[0]
    block = 2 * shard
    width = q.shape[1]
    chunks = width // CHUNK
    heads = CHUNK // HD

    def slot(yy, xx, hh, cc):
        return ((lax.rem(yy + 4, 4) * 4 + lax.rem(xx + 4, 4)) * 2 + hh) * 2 + cc

    sibling = (slot(y, x, zhi, 1 - core), zlo)
    far = (slot(y, x, 1 - zhi, core), zlo)
    before = (lax.rem(seq + 63, 64), zlo)
    after = (lax.rem(seq + 1, 64), zlo)
    flip1 = zlo + 1 - 2 * lax.rem(zlo, 2)
    flip2 = lax.rem(zlo + 2, 4)
    side1 = (seq, flip1)
    side2 = (seq, flip2)

    def place(i, j):
        return y + core * i + (1 - core) * j, x + (1 - core) * i + core * j

    def at(f, i, j):
        yy, xx = place(i, j)
        return slot(yy, xx, f, core)

    def near(i, j):
        yy, xx = place(i, j)
        return (slot(yy, xx, zhi, core), zlo)

    loads = [
        pltpu.make_async_copy(src, dst, local_sem.at[n])
        for n, (src, dst) in enumerate(
            [(dl_hbm, dl), (q_hbm, q), (k_hbm, k), (v_hbm, v), (ao_hbm, ao), (log_hbm, logs)]
        )
    ]

    def w_rows(s):
        return wbuf.at[pl.ds(pl.multiple_of(s * shard, 16), shard)]

    own = pltpu.make_async_copy(w_hbm, w_rows(seq), w_recv.at[seq])
    own.start()
    for c in loads:
        c.start()

    barrier = pltpu.get_barrier_semaphore()
    partners = [sibling, far, before, after, side1, side2]
    for d in (1, -1):
        partners += [near(d, 0), near(0, d)]
    for p in partners:
        pl.semaphore_signal(barrier, inc=1, device_id=p, device_id_type=MESH)
    pl.semaphore_wait(barrier, len(partners))

    w_sends = []

    def w_copy(s, device, n):
        return pltpu.make_async_remote_copy(
            w_rows(s), w_rows(s), w_send.at[n], w_recv.at[s],
            device_id=device, device_id_type=MESH,
        )

    def send_w(s, device):
        c = w_copy(s, device, len(w_sends))
        c.start()
        w_sends.append(c)

    def wait_w(s):
        w_copy(s, sibling, 0).wait_recv()

    own.wait()
    send_w(seq, far)
    zf, zg = zhi, 1 - zhi

    def begin(f):
        s = at(f, 0, 0)
        for d in (1, -1):
            send_w(s, near(d, 0))
        for d in (1, -1):
            send_w(s, near(0, d))
        send_w(s, sibling)

    def spread(f, i):
        s = at(f, i, 0)
        for d in (1, -1):
            send_w(s, near(0, d))
        send_w(s, sibling)

    def first_near(f):
        wait_w(at(f, 1, 0))
        wait_w(at(f, -1, 0))
        step = 1 - 2 * f
        send_w(at(f, -step, 0), near(step, 0))
        spread(f, 1)
        spread(f, -1)

    def first_far(f):
        wait_w(at(f, 2, 0))
        spread(f, 2)

    def second_near(f, i):
        for d in (1, -1):
            wait_w(at(f, i, d))
        d = 1 if i in (0, 1) else -1
        send_w(at(f, i, -d), near(0, d))
        for d in (1, -1):
            send_w(at(f, i, d), sibling)

    def second_far(f, i):
        wait_w(at(f, i, 2))
        send_w(at(f, i, 2), sibling)

    def rows_of(b):
        return pl.ds(pl.multiple_of(b * block, 16), block)

    def one_copy(j, b):
        return pltpu.make_async_remote_copy(
            send1.at[j, rows_of(b)], recv1.at[j, rows_of(b)], one_send.at[j, b], one_recv.at[j, b],
            device_id=side1, device_id_type=MESH,
        )

    def two_copy(b):
        return pltpu.make_async_remote_copy(
            send2.at[rows_of(b)], recv2.at[rows_of(b)], two_send.at[b], two_recv.at[b],
            device_id=side2, device_id_type=MESH,
        )

    def do_copy(b):
        return pltpu.make_async_remote_copy(
            do.at[rows_of(b)], do_next.at[rows_of(b)], do_send.at[b], do_rsem.at[b],
            device_id=before, device_id_type=MESH,
        )

    def group(f, d):
        h = lax.rem(y + d + 4, 4)
        for xx in range(4):
            wait_w(slot(h, xx, f, 1 - core))
        mine = lax.rem(h + zlo, 2) == 0

        def product(b):
            rows = pl.ds(pl.multiple_of(h * width + b * block, 16), block)
            return dot(wbuf[rows, :], dl[...], NT)

        @pl.when(mine)
        def _():
            j = jnp.where(h == zlo, 0, 1)

            def body(n, carry):
                b = 2 * n + f
                keep[j, rows_of(b)] = product(b)
                return carry

            lax.fori_loop(0, 4, body, 0)

        @pl.when(jnp.logical_not(mine))
        def _():
            j = jnp.where(h == flip1, 0, 1)

            def body(n, carry):
                b = 2 * n + f
                send1[j, rows_of(b)] = product(b).astype(jnp.bfloat16)
                one_copy(j, b).start()
                return carry

            lax.fori_loop(0, 4, body, 0)

    def combine(f):
        def body(n, carry):
            b = 2 * n + f
            one_copy(1, b).wait_recv()
            both = keep[1, rows_of(b)] + recv1[1, rows_of(b)].astype(jnp.float32)
            send2[rows_of(b)] = both.astype(jnp.bfloat16)
            two_copy(b).start()
            return carry

        lax.fori_loop(0, 4, body, 0)

    def finish(f):
        def body(n, carry):
            b = 2 * n + f
            one_copy(0, b).wait_recv()
            two_copy(b).wait_recv()
            total = keep[0, rows_of(b)] + recv1[0, rows_of(b)].astype(jnp.float32)
            total = total + recv2[rows_of(b)].astype(jnp.float32)
            do[rows_of(b)] = total.astype(jnp.bfloat16)
            do_copy(b).start()
            return carry

        lax.fori_loop(0, 4, body, 0)

    begin(zf)
    first_near(zf)
    first_far(zf)
    second_near(zf, 0)
    second_near(zf, 1)
    wait_w(at(zg, 0, 0))
    begin(zg)
    for c in loads:
        c.wait()
    q_copy = pltpu.make_async_remote_copy(
        q, q_next, q_send.at[0], q_rsem.at[0], device_id=before, device_id_type=MESH
    )
    log_copy = pltpu.make_async_remote_copy(
        logs, log_next, q_send.at[1], q_rsem.at[1], device_id=before, device_id_type=MESH
    )
    q_copy.start()
    log_copy.start()
    second_near(zf, -1)
    second_near(zf, 2)
    second_far(zf, 0)
    group(zf, 0)
    first_near(zg)
    second_far(zf, 1)
    second_far(zf, -1)
    group(zf, 1)
    group(zf, -1)
    first_far(zg)
    second_far(zf, 2)
    group(zf, 2)
    second_near(zg, 0)
    second_near(zg, 1)

    def turn(t, carry):
        c = pl.ds(pl.multiple_of(t * HD, HD), HD)
        ao_t[c, :] = ao[:, c].T
        return carry

    lax.fori_loop(0, width // HD, turn, 0)
    combine(zf)
    second_near(zg, -1)
    second_near(zg, 2)
    second_far(zg, 0)
    group(zg, 0)
    second_far(zg, 1)
    second_far(zg, -1)
    group(zg, 1)
    group(zg, -1)
    finish(zf)
    second_far(zg, 2)
    group(zg, 2)
    combine(zg)
    finish(zg)

    def delta_copy(t):
        return pltpu.make_async_remote_copy(
            delta.at[t], delta_next.at[t], delta_send.at[t], delta_rsem.at[t],
            device_id=before, device_id_type=MESH,
        )

    def back_copy(t):
        return pltpu.make_async_remote_copy(
            dq_send.at[t], dq_recv.at[t], back_send.at[t], back_rsem.at[t],
            device_id=after, device_id_type=MESH,
        )

    def cols(t, n):
        return pl.ds(pl.multiple_of(t * CHUNK + n * HD, HD), HD)

    def row_delta(t, carry):
        for n in range(heads):
            c = cols(t, n)
            prod = do[c, :].astype(jnp.float32) * ao_t[c, :].astype(jnp.float32)
            row = jnp.sum(prod, axis=0, keepdims=True)
            delta[t, n * 4:(n + 1) * 4, :] = jnp.broadcast_to(row, (4, row.shape[1]))
        delta_copy(t).start()
        return carry

    lax.fori_loop(0, chunks, row_delta, 0)

    rows_i = q.shape[0]
    key_at = lax.broadcasted_iota(jnp.int32, (rows_i, rows_i), 0)
    query_at = lax.broadcasted_iota(jnp.int32, (rows_i, rows_i), 1)

    def head_grads(qh, kh, vh, doh, log_row, delta_row, allowed):
        score = dot(kh, qh, NT) * SCALE - log_row
        probs = jnp.exp(jnp.where(allowed, score, MASKED))
        g_value = dot(probs.astype(jnp.bfloat16), doh, NT)
        g_probs = dot(vh, doh, NN)
        low = (probs * (g_probs - delta_row)).astype(jnp.bfloat16)
        g_key = dot(low, qh, NN) * SCALE
        g_query = dot(low, kh, TN) * SCALE
        return g_query, g_key, g_value

    def diagonal(t, carry):
        for n in range(heads):
            c = cols(t, n)
            part = slice(n * HD, (n + 1) * HD)
            g = head_grads(
                q[:, c], k[:, c], v[:, c], do[c, :],
                logs[pl.ds(t * heads + n, 1), :], delta[t, n * 4:n * 4 + 1, :],
                key_at <= query_at,
            )
            dq_acc[t, :, part], dk_acc[t, :, part], dv_acc[t, :, part] = g
        return carry

    lax.fori_loop(0, chunks, diagonal, 0)

    q_copy.wait_recv()
    log_copy.wait_recv()
    limit = jnp.where(seq < 63, rows_i, 0)
    arrived = 0
    for t in range(chunks):
        needed = -(-(t + 1) * CHUNK // block)
        for b in range(arrived, needed):
            do_copy(b).wait_recv()
        arrived = needed
        delta_copy(t).wait_recv()
        for n in range(heads):
            c = slice(t * CHUNK + n * HD, t * CHUNK + (n + 1) * HD)
            part = slice(n * HD, (n + 1) * HD)
            g_query, g_key, g_value = head_grads(
                q_next[:, c], k[:, c], v[:, c], do_next[c, :],
                log_next[t * heads + n:t * heads + n + 1, :], delta_next[t, n * 4:n * 4 + 1, :],
                key_at < limit,
            )
            dq_send[t, :, part] = g_query.astype(jnp.bfloat16)
            dk_ref[:, c] = (dk_acc[t, :, part] + g_key).astype(jnp.bfloat16)
            dv_ref[:, c] = (dv_acc[t, :, part] + g_value).astype(jnp.bfloat16)
        back_copy(t).start()

    def close(t, carry):
        back_copy(t).wait_recv()
        c = pl.ds(pl.multiple_of(t * CHUNK, CHUNK), CHUNK)
        dq_ref[:, c] = (dq_acc[t] + dq_recv[t].astype(jnp.float32)).astype(jnp.bfloat16)
        return carry

    lax.fori_loop(0, chunks, close, 0)

    for c in w_sends:
        c.wait_send()
    q_copy.wait_send()
    log_copy.wait_send()

    def drain_sums(b, carry):
        one_copy(0, b).wait_send()
        one_copy(1, b).wait_send()
        two_copy(b).wait_send()
        do_copy(b).wait_send()
        return carry

    lax.fori_loop(0, width // block, drain_sums, 0)

    def drain(t, carry):
        delta_copy(t).wait_send()
        back_copy(t).wait_send()
        return carry

    lax.fori_loop(0, chunks, drain, 0)


def on_device(query_rows, key_rows, value_rows, attn_out, log_total, d_layer, w_output):
    rows, width = query_rows.shape
    n_heads = log_total.shape[0]
    chunks = width // CHUNK
    seqs = lax.axis_size("seq")
    bf, f32 = jnp.bfloat16, jnp.float32
    full = (rows, width)
    cut = (chunks, rows, CHUNK)
    dma = pltpu.SemaphoreType.DMA
    vm = pltpu.VMEM
    blocks = width // (2 * w_output.shape[0])
    turned = (width, rows)
    scratch = [
        vm((w_output.shape[0] * seqs, width), bf),
        vm(full, bf), vm(full, bf), vm(full, bf), vm(full, bf), vm(full, bf), vm(turned, bf),
        vm((n_heads, rows), f32), vm(full, bf), vm((n_heads, rows), f32),
        vm((2,) + turned, f32), vm((2,) + turned, bf), vm((2,) + turned, bf),
        vm(turned, bf), vm(turned, bf), vm(turned, bf), vm(turned, bf),
        vm((chunks, 8, rows), f32), vm((chunks, 8, rows), f32),
        vm(cut, f32), vm(cut, f32), vm(cut, f32), vm(cut, bf), vm(cut, bf),
        dma((6,)), dma((64,)), dma((64,)), dma((2, blocks)), dma((2, blocks)),
        dma((blocks,)), dma((blocks,)), dma((2,)), dma((2,)),
        dma((blocks,)), dma((blocks,)), dma((chunks,)), dma((chunks,)),
        dma((chunks,)), dma((chunks,)),
    ]
    out = jax.ShapeDtypeStruct(full, bf)
    return pl.pallas_call(
        kernel,
        out_shape=(out, out, out),
        in_specs=[pl.BlockSpec(memory_space=pl.ANY)] * 7,
        out_specs=[pl.BlockSpec(memory_space=pltpu.VMEM)] * 3,
        scratch_shapes=scratch,
        compiler_params=pltpu.CompilerParams(
            collective_id=0, has_side_effects=True, vmem_limit_bytes=56 * 2**20
        ),
    )(query_rows, key_rows, value_rows, attn_out, log_total, d_layer, w_output)


def solution(mesh):
    spec = P("seq", "head")
    return jax.shard_map(
        on_device,
        mesh=mesh,
        in_specs=(spec, spec, spec, spec, P("head", "seq"), spec, spec),
        out_specs=(spec, spec, spec),
        check_vma=False,
    )
```

```python
import functools

import jax
import jax.numpy as jnp
from jax import lax
from jax.experimental import pallas as pl
from jax.experimental.pallas import tpu as pltpu
from jax.sharding import PartitionSpec as P

HD = 128
SCALE = HD ** (-0.5)
MASKED = -1e30
CHUNK = 256
MESH = pl.DeviceIdType.MESH
NT = (((1,), (1,)), ((), ()))
NN = (((1,), (0,)), ((), ()))
TN = (((0,), (0,)), ((), ()))


def dot(a, b, dims):
    return lax.dot_general(a, b, dims, preferred_element_type=jnp.float32)


def kernel(
    q_hbm, k_hbm, v_hbm, ao_hbm, log_hbm, dl_hbm, w_hbm,
    dq_ref, dk_ref, dv_ref,
    wbuf, dl, q, k, v, ao, ao_t, logs, q_next, log_next,
    keep, send1, recv1, send2, do, do_parts, do_next, next_parts, delta, delta_next,
    dq_acc, dk_acc, dv_acc, dq_send, dq_recv,
    local_sem, w_send, w_recv, dl_sem, one_send, one_recv, two_send, two_recv,
    q_send, q_rsem, do_send, do_rsem, delta_send, delta_rsem, back_send, back_rsem,
):
    seq = lax.axis_index("seq")
    zlo = lax.axis_index("head")
    core = lax.rem(seq, 2)
    zhi = lax.rem(seq // 2, 2)
    x = lax.rem(seq // 4, 4)
    y = seq // 16
    shard = w_hbm.shape[0]
    part = 4 * shard
    width = q.shape[1]
    chunks = width // CHUNK
    heads = CHUNK // HD

    def device(yy, xx, hh, cc):
        return ((lax.rem(yy + 4, 4) * 4 + lax.rem(xx + 4, 4)) * 2 + hh) * 2 + cc

    flip1 = zlo + 1 - 2 * lax.rem(zlo, 2)
    flip2 = lax.rem(zlo + 2, 4)
    sibling = (device(y, x, zhi, 1 - core), zlo)
    far = (device(y, x, 1 - zhi, core), zlo)
    cross1 = (device(y, x, zhi, 1 - core), flip1)
    cross2 = (device(y, x, 1 - zhi, 1 - core), flip1)
    before = (lax.rem(seq + 63, 64), zlo)
    after = (lax.rem(seq + 1, 64), zlo)
    side1 = (seq, flip1)
    side2 = (seq, flip2)

    pair = zlo // 2
    half = lax.rem(zlo, 2)
    home = core == half

    def slot(yy, c, f, xx):
        return ((lax.rem(yy + 4, 4) * 2 + c) * 2 + f) * 4 + lax.rem(xx + 4, 4)

    def place(i, j):
        return y + core * i + (1 - core) * j, x + (1 - core) * i + core * j

    def at(f, i, j):
        yy, xx = place(i, j)
        return slot(yy, core, f, xx)

    def near(i, j):
        yy, xx = place(i, j)
        return (device(yy, xx, zhi, core), zlo)

    loads = [
        pltpu.make_async_copy(src, dst, local_sem.at[n])
        for n, (src, dst) in enumerate(
            [(dl_hbm, dl.at[half]), (q_hbm, q), (k_hbm, k), (v_hbm, v), (ao_hbm, ao), (log_hbm, logs)]
        )
    ]

    def w_rows(s):
        return wbuf.at[pl.ds(pl.multiple_of(s * shard, 16), shard)]

    own_slot = slot(y, half, zhi, x)

    @pl.when(home)
    def _():
        pltpu.make_async_copy(w_hbm, w_rows(own_slot), w_recv.at[own_slot]).start()

    for c in loads:
        c.start()

    barrier = pltpu.get_barrier_semaphore()
    partners = [sibling, far, cross1, cross2, before, after, side1, side2]
    for d in (1, -1):
        partners += [near(d, 0), near(0, d)]
    for p in partners:
        pl.semaphore_signal(barrier, inc=1, device_id=p, device_id_type=MESH)
    pl.semaphore_wait(barrier, len(partners))

    w_sends = []

    def w_copy(s, device, n):
        return pltpu.make_async_remote_copy(
            w_rows(s), w_rows(s), w_send.at[n], w_recv.at[s],
            device_id=device, device_id_type=MESH,
        )

    def send_w(s, device):
        c = w_copy(s, device, len(w_sends))
        c.start()
        w_sends.append(c)

    def wait_w(s):
        w_copy(s, sibling, 0).wait_recv()

    def z_move(n, device):
        return pltpu.make_async_remote_copy(
            w_hbm, w_rows(own_slot), w_send.at[n], w_recv.at[own_slot],
            device_id=device, device_id_type=MESH,
        )

    @pl.when(home)
    def _():
        z_move(62, far).start()

    @pl.when(jnp.logical_not(home))
    def _():
        z_move(62, cross1).start()
        z_move(63, cross2).start()

    zf, zg = zhi, 1 - zhi

    def begin(f):
        s = at(f, 0, 0)
        for d in (1, -1):
            send_w(s, near(d, 0))
        for d in (1, -1):
            send_w(s, near(0, d))
        send_w(s, sibling)

    def spread(f, i):
        s = at(f, i, 0)
        for d in (1, -1):
            send_w(s, near(0, d))
        send_w(s, sibling)

    def first_near(f):
        wait_w(at(f, 1, 0))
        wait_w(at(f, -1, 0))
        step = 1 - 2 * f
        send_w(at(f, -step, 0), near(step, 0))
        spread(f, 1)
        spread(f, -1)

    def first_far(f):
        wait_w(at(f, 2, 0))
        spread(f, 2)

    def second_near(f, i):
        for d in (1, -1):
            wait_w(at(f, i, d))
        d = 1 if i in (0, 1) else -1
        send_w(at(f, i, -d), near(0, d))
        for d in (1, -1):
            send_w(at(f, i, d), sibling)

    def second_far(f, i):
        wait_w(at(f, i, 2))
        send_w(at(f, i, 2), sibling)

    def one_copy(j, f):
        return pltpu.make_async_remote_copy(
            send1.at[j, f], recv1.at[j, f], one_send.at[j, f], one_recv.at[j, f],
            device_id=side2, device_id_type=MESH,
        )

    def two_copy(f):
        return pltpu.make_async_remote_copy(
            send2.at[f], do_parts.at[half, f], two_send.at[f], two_recv.at[f],
            device_id=side1, device_id_type=MESH,
        )

    def two_arrival(f):
        return pltpu.make_async_remote_copy(
            send2.at[f], do_parts.at[1 - half, f], two_send.at[f], two_recv.at[f],
            device_id=side1, device_id_type=MESH,
        )

    def do_copy(b, f):
        return pltpu.make_async_remote_copy(
            do_parts.at[b, f], next_parts.at[b, f], do_send.at[b, f], do_rsem.at[b, f],
            device_id=before, device_id_type=MESH,
        )

    def group(f, d):
        h = lax.rem(y + d + 4, 4)
        for xx in range(4):
            wait_w(slot(h, 1 - core, f, xx))
        mine = h // 2 == pair
        j = lax.rem(h, 2)

        def product():
            total = 0.0
            for c in range(2):
                rows = pl.ds(pl.multiple_of(slot(h, c, f, 0) * shard, 16), part)
                total += dot(wbuf[rows, :], dl[c], NT)
            return total

        @pl.when(mine)
        def _():
            keep[j, f] = product()

        @pl.when(jnp.logical_not(mine))
        def _():
            send1[j, f] = product().astype(jnp.bfloat16)
            one_copy(j, f).start()

    def combine(f, d):
        h = lax.rem(y + d + 4, 4)
        j = lax.rem(h, 2)

        def total():
            one_copy(j, f).wait_recv()
            return (keep[j, f] + recv1[j, f].astype(jnp.float32)).astype(jnp.bfloat16)

        @pl.when(h == zlo)
        def _():
            do_parts[half, f] = total()
            do_copy(half, f).start()

        @pl.when(h == flip1)
        def _():
            send2[f] = total()
            two_copy(f).start()

    def forward(f, d):
        h = lax.rem(y + d + 4, 4)

        @pl.when(h == zlo)
        def _():
            two_arrival(f).wait_recv()
            do_copy(1 - half, f).start()

    def arrange(parts, whole):
        for m in range(16):
            xx, f, b = m // 4, m // 2 % 2, m % 2
            whole[m * shard:(m + 1) * shard, :] = parts[b, f, xx * shard:(xx + 1) * shard, :]

    wait_w(at(zf, 0, 0))
    begin(zf)
    first_near(zf)
    dl_copy = pltpu.make_async_remote_copy(
        dl_hbm, dl.at[half], dl_sem.at[0], dl_sem.at[1], device_id=side1, device_id_type=MESH
    )
    dl_arrival = pltpu.make_async_remote_copy(
        dl_hbm, dl.at[1 - half], dl_sem.at[0], dl_sem.at[1], device_id=side1, device_id_type=MESH
    )
    dl_copy.start()
    first_far(zf)
    second_near(zf, 0)
    second_near(zf, 1)
    wait_w(at(zg, 0, 0))
    begin(zg)
    for c in loads:
        c.wait()
    q_copy = pltpu.make_async_remote_copy(
        q, q_next, q_send.at[0], q_rsem.at[0], device_id=before, device_id_type=MESH
    )
    log_copy = pltpu.make_async_remote_copy(
        logs, log_next, q_send.at[1], q_rsem.at[1], device_id=before, device_id_type=MESH
    )
    q_copy.start()
    log_copy.start()
    second_near(zf, -1)
    second_near(zf, 2)
    second_far(zf, 0)
    first_near(zg)
    dl_arrival.wait_recv()
    group(zf, 0)
    second_far(zf, 1)
    second_far(zf, -1)
    group(zf, 1)
    group(zf, -1)
    first_far(zg)
    second_far(zf, 2)
    group(zf, 2)
    second_near(zg, 0)
    second_near(zg, 1)
    combine(zf, 0)
    combine(zf, 1)

    def turn(t, carry):
        c = pl.ds(pl.multiple_of(t * HD, HD), HD)
        ao_t[c, :] = ao[:, c].T
        return carry

    lax.fori_loop(0, width // HD, turn, 0)
    second_near(zg, -1)
    second_near(zg, 2)
    combine(zf, -1)
    combine(zf, 2)
    second_far(zg, 0)
    group(zg, 0)
    forward(zf, 0)
    forward(zf, 1)
    second_far(zg, 1)
    second_far(zg, -1)
    group(zg, 1)
    group(zg, -1)
    forward(zf, -1)
    forward(zf, 2)
    combine(zg, 0)
    second_far(zg, 2)
    group(zg, 2)
    combine(zg, 1)
    combine(zg, -1)
    forward(zg, 0)
    forward(zg, 1)
    combine(zg, 2)
    forward(zg, -1)
    forward(zg, 2)
    arrange(do_parts, do)

    def delta_copy(t):
        return pltpu.make_async_remote_copy(
            delta.at[t], delta_next.at[t], delta_send.at[t], delta_rsem.at[t],
            device_id=before, device_id_type=MESH,
        )

    def back_copy(t):
        return pltpu.make_async_remote_copy(
            dq_send.at[t], dq_recv.at[t], back_send.at[t], back_rsem.at[t],
            device_id=after, device_id_type=MESH,
        )

    def cols(t, n):
        return pl.ds(pl.multiple_of(t * CHUNK + n * HD, HD), HD)

    def row_delta(t, carry):
        for n in range(heads):
            c = cols(t, n)
            prod = do[c, :].astype(jnp.float32) * ao_t[c, :].astype(jnp.float32)
            row = jnp.sum(prod, axis=0, keepdims=True)
            delta[t, n * 4:(n + 1) * 4, :] = jnp.broadcast_to(row, (4, row.shape[1]))
        delta_copy(t).start()
        return carry

    lax.fori_loop(0, chunks, row_delta, 0)

    rows_i = q.shape[0]
    key_at = lax.broadcasted_iota(jnp.int32, (rows_i, rows_i), 0)
    query_at = lax.broadcasted_iota(jnp.int32, (rows_i, rows_i), 1)

    def head_grads(qh, kh, vh, doh, log_row, delta_row, allowed):
        score = dot(kh, qh, NT) * SCALE - log_row
        probs = jnp.exp(jnp.where(allowed, score, MASKED))
        g_value = dot(probs.astype(jnp.bfloat16), doh, NT)
        g_probs = dot(vh, doh, NN)
        low = (probs * (g_probs - delta_row)).astype(jnp.bfloat16)
        g_key = dot(low, qh, NN) * SCALE
        g_query = dot(low, kh, TN) * SCALE
        return g_query, g_key, g_value

    for t in range(chunks):
        for n in range(heads):
            c = slice(t * CHUNK + n * HD, t * CHUNK + (n + 1) * HD)
            own = slice(n * HD, (n + 1) * HD)
            g = head_grads(
                q[:, c], k[:, c], v[:, c], do[c, :],
                logs[t * heads + n:t * heads + n + 1, :], delta[t, n * 4:n * 4 + 1, :],
                key_at <= query_at,
            )
            dq_acc[t, :, own], dk_acc[t, :, own], dv_acc[t, :, own] = g

    q_copy.wait_recv()
    log_copy.wait_recv()
    limit = jnp.where(seq < 63, rows_i, 0)
    for b in range(2):
        for f in range(2):
            do_copy(b, f).wait_recv()
    arrange(next_parts, do_next)
    for t in range(chunks):
        delta_copy(t).wait_recv()
        for n in range(heads):
            c = slice(t * CHUNK + n * HD, t * CHUNK + (n + 1) * HD)
            own = slice(n * HD, (n + 1) * HD)
            g_query, g_key, g_value = head_grads(
                q_next[:, c], k[:, c], v[:, c], do_next[c, :],
                log_next[t * heads + n:t * heads + n + 1, :], delta_next[t, n * 4:n * 4 + 1, :],
                key_at < limit,
            )
            dq_send[t, :, own] = g_query.astype(jnp.bfloat16)
            dk_ref[:, c] = (dk_acc[t, :, own] + g_key).astype(jnp.bfloat16)
            dv_ref[:, c] = (dv_acc[t, :, own] + g_value).astype(jnp.bfloat16)
        back_copy(t).start()

    def close(t, carry):
        back_copy(t).wait_recv()
        c = pl.ds(pl.multiple_of(t * CHUNK, CHUNK), CHUNK)
        dq_ref[:, c] = (dq_acc[t] + dq_recv[t].astype(jnp.float32)).astype(jnp.bfloat16)
        return carry

    lax.fori_loop(0, chunks, close, 0)

    for c in w_sends:
        c.wait_send()
    z_move(62, far).wait_send()

    @pl.when(jnp.logical_not(home))
    def _():
        z_move(63, cross2).wait_send()

    dl_copy.wait_send()
    q_copy.wait_send()
    log_copy.wait_send()

    for b in range(2):
        two_copy(b).wait_send()
        for f in range(2):
            one_copy(b, f).wait_send()
            do_copy(b, f).wait_send()

    def drain(t, carry):
        delta_copy(t).wait_send()
        back_copy(t).wait_send()
        return carry

    lax.fori_loop(0, chunks, drain, 0)


def on_device(query_rows, key_rows, value_rows, attn_out, log_total, d_layer, w_output):
    rows, width = query_rows.shape
    n_heads = log_total.shape[0]
    chunks = width // CHUNK
    seqs = lax.axis_size("seq")
    bf, f32 = jnp.bfloat16, jnp.float32
    full = (rows, width)
    cut = (chunks, rows, CHUNK)
    dma = pltpu.SemaphoreType.DMA
    vm = pltpu.VMEM
    part = 4 * w_output.shape[0]
    turned = (width, rows)
    scratch = [
        vm((w_output.shape[0] * seqs, width), bf),
        vm((2,) + full, bf), vm(full, bf), vm(full, bf), vm(full, bf), vm(full, bf), vm(turned, bf),
        vm((n_heads, rows), f32), vm(full, bf), vm((n_heads, rows), f32),
        vm((2, 2, part, rows), f32), vm((2, 2, part, rows), bf), vm((2, 2, part, rows), bf),
        vm((2, part, rows), bf), vm(turned, bf), vm((2, 2, part, rows), bf),
        vm(turned, bf), vm((2, 2, part, rows), bf),
        vm((chunks, 8, rows), f32), vm((chunks, 8, rows), f32),
        vm(cut, f32), vm(cut, f32), vm(cut, f32), vm(cut, bf), vm(cut, bf),
        dma((6,)), dma((64,)), dma((64,)), dma((2,)), dma((2, 2)), dma((2, 2)),
        dma((2,)), dma((2,)), dma((2,)), dma((2,)),
        dma((2, 2)), dma((2, 2)), dma((chunks,)), dma((chunks,)),
        dma((chunks,)), dma((chunks,)),
    ]
    out = jax.ShapeDtypeStruct(full, bf)
    return pl.pallas_call(
        kernel,
        out_shape=(out, out, out),
        in_specs=[pl.BlockSpec(memory_space=pl.ANY)] * 7,
        out_specs=[pl.BlockSpec(memory_space=pltpu.VMEM)] * 3,
        scratch_shapes=scratch,
        compiler_params=pltpu.CompilerParams(
            collective_id=0, has_side_effects=True, vmem_limit_bytes=56 * 2**20
        ),
    )(query_rows, key_rows, value_rows, attn_out, log_total, d_layer, w_output)


def solution(mesh):
    spec = P("seq", "head")
    return jax.shard_map(
        on_device,
        mesh=mesh,
        in_specs=(spec, spec, spec, spec, P("head", "seq"), spec, spec),
        out_specs=(spec, spec, spec),
        check_vma=False,
    )
```

```python
import functools

import jax
import jax.numpy as jnp
from jax import lax
from jax.experimental import pallas as pl
from jax.experimental.pallas import tpu as pltpu
from jax.sharding import PartitionSpec as P

HD = 128
SCALE = HD ** (-0.5)
MASKED = -1e30
CHUNK = 256
MESH = pl.DeviceIdType.MESH
NT = (((1,), (1,)), ((), ()))
NN = (((1,), (0,)), ((), ()))
TN = (((0,), (0,)), ((), ()))


def dot(a, b, dims):
    return lax.dot_general(a, b, dims, preferred_element_type=jnp.float32)


def kernel(
    q_hbm, k_hbm, v_hbm, ao_hbm, log_hbm, dl_hbm, w_hbm,
    dq_ref, dk_ref, dv_ref,
    wbuf, dl, q, k, v, ao, ao_t, logs, q_next, log_next,
    keep, send1, recv1, send2, do, do_parts, do_next, next_parts, delta, delta_next,
    dq_acc, dk_acc, dv_acc, dq_send, dq_recv,
    local_sem, w_send, w_recv, dl_sem, one_send, one_recv, two_send, two_recv, side_send,
    q_send, q_rsem, do_send, do_rsem, delta_send, delta_rsem, back_send, back_rsem,
):
    seq = lax.axis_index("seq")
    zlo = lax.axis_index("head")
    core = lax.rem(seq, 2)
    zhi = lax.rem(seq // 2, 2)
    x = lax.rem(seq // 4, 4)
    y = seq // 16
    shard = w_hbm.shape[0]
    part = 4 * shard
    width = q.shape[1]
    chunks = width // CHUNK
    heads = CHUNK // HD

    def device(yy, xx, hh, cc):
        return ((lax.rem(yy + 4, 4) * 4 + lax.rem(xx + 4, 4)) * 2 + hh) * 2 + cc

    flip1 = zlo + 1 - 2 * lax.rem(zlo, 2)
    flip2 = lax.rem(zlo + 2, 4)
    sibling = (device(y, x, zhi, 1 - core), zlo)
    far = (device(y, x, 1 - zhi, core), zlo)
    cross1 = (device(y, x, zhi, 1 - core), flip1)
    cross2 = (device(y, x, 1 - zhi, 1 - core), flip1)
    before = (lax.rem(seq + 63, 64), zlo)
    after = (lax.rem(seq + 1, 64), zlo)
    side1 = (seq, flip1)
    side2 = (seq, flip2)
    before1 = (lax.rem(seq + 63, 64), flip1)
    after1 = (lax.rem(seq + 1, 64), flip1)

    pair = zlo // 2
    half = lax.rem(zlo, 2)
    home = core == half

    def slot(yy, c, f, xx):
        return ((lax.rem(yy + 4, 4) * 2 + c) * 2 + f) * 4 + lax.rem(xx + 4, 4)

    def place(i, j):
        return y + core * i + (1 - core) * j, x + (1 - core) * i + core * j

    def at(f, i, j):
        yy, xx = place(i, j)
        return slot(yy, core, f, xx)

    def near(i, j):
        yy, xx = place(i, j)
        return (device(yy, xx, zhi, core), zlo)

    loads = [
        pltpu.make_async_copy(src, dst, local_sem.at[n])
        for n, (src, dst) in enumerate(
            [(dl_hbm, dl.at[half]), (q_hbm, q), (k_hbm, k), (v_hbm, v), (ao_hbm, ao), (log_hbm, logs)]
        )
    ]

    def w_rows(s):
        return wbuf.at[pl.ds(pl.multiple_of(s * shard, 16), shard)]

    own_slot = slot(y, half, zhi, x)

    @pl.when(home)
    def _():
        pltpu.make_async_copy(w_hbm, w_rows(own_slot), w_recv.at[own_slot]).start()

    for c in loads:
        c.start()

    barrier = pltpu.get_barrier_semaphore()
    partners = [sibling, far, cross1, cross2, before, after, before1, after1, side1, side2]
    for d in (1, -1):
        partners += [near(d, 0), near(0, d)]
    partners += [near(2, 0)]
    for p in partners:
        pl.semaphore_signal(barrier, inc=1, device_id=p, device_id_type=MESH)
    pl.semaphore_wait(barrier, len(partners))

    w_sends = []

    def w_copy(s, device, n):
        return pltpu.make_async_remote_copy(
            w_rows(s), w_rows(s), w_send.at[n], w_recv.at[s],
            device_id=device, device_id_type=MESH,
        )

    def send_w(s, device):
        c = w_copy(s, device, len(w_sends))
        c.start()
        w_sends.append(c)

    def wait_w(s):
        w_copy(s, sibling, 0).wait_recv()

    def z_move(n, device):
        return pltpu.make_async_remote_copy(
            w_hbm, w_rows(own_slot), w_send.at[n], w_recv.at[own_slot],
            device_id=device, device_id_type=MESH,
        )

    @pl.when(home)
    def _():
        z_move(62, far).start()

    @pl.when(jnp.logical_not(home))
    def _():
        z_move(62, cross1).start()
        z_move(63, cross2).start()

    zf, zg = zhi, 1 - zhi

    def begin(f):
        s = at(f, 0, 0)
        for d in (1, -1, 2):
            send_w(s, near(d, 0))
        for d in (1, -1):
            send_w(s, near(0, d))
        send_w(s, sibling)

    def spread(f, i):
        s = at(f, i, 0)
        for d in (1, -1):
            send_w(s, near(0, d))
        send_w(s, sibling)

    def first_near(f):
        wait_w(at(f, 1, 0))
        wait_w(at(f, -1, 0))
        spread(f, 1)
        spread(f, -1)

    def first_far(f):
        wait_w(at(f, 2, 0))
        spread(f, 2)

    def second_near(f, i):
        for d in (1, -1):
            wait_w(at(f, i, d))
        d = 1 if i in (0, 1) else -1
        send_w(at(f, i, -d), near(0, d))
        for d in (1, -1):
            send_w(at(f, i, d), sibling)

    def second_far(f, i):
        wait_w(at(f, i, 2))
        send_w(at(f, i, 2), sibling)

    def one_copy(j, f):
        return pltpu.make_async_remote_copy(
            send1.at[j, f], recv1.at[j, f], one_send.at[j, f], one_recv.at[j, f],
            device_id=side2, device_id_type=MESH,
        )

    def two_copy(f):
        return pltpu.make_async_remote_copy(
            send2.at[f], do_parts.at[half, f], two_send.at[f], two_recv.at[f],
            device_id=side1, device_id_type=MESH,
        )

    def two_arrival(f):
        return pltpu.make_async_remote_copy(
            send2.at[f], do_parts.at[1 - half, f], two_send.at[f], two_recv.at[f],
            device_id=side1, device_id_type=MESH,
        )

    def do_copy(b, f):
        return pltpu.make_async_remote_copy(
            do_parts.at[b, f], next_parts.at[b, f], do_send.at[f], do_rsem.at[b, f],
            device_id=before, device_id_type=MESH,
        )

    def side_copy(f):
        return pltpu.make_async_remote_copy(
            send2.at[f], next_parts.at[half, f], side_send.at[f], do_rsem.at[half, f],
            device_id=before1, device_id_type=MESH,
        )

    def group(f, d):
        h = lax.rem(y + d + 4, 4)
        for xx in range(4):
            wait_w(slot(h, 1 - core, f, xx))
        mine = h // 2 == pair
        j = lax.rem(h, 2)

        def product():
            total = 0.0
            for c in range(2):
                rows = pl.ds(pl.multiple_of(slot(h, c, f, 0) * shard, 16), part)
                total += dot(wbuf[rows, :], dl[c], NT)
            return total

        @pl.when(mine)
        def _():
            keep[j, f] = product()

        @pl.when(jnp.logical_not(mine))
        def _():
            send1[j, f] = product().astype(jnp.bfloat16)
            one_copy(j, f).start()

    def combine(f, d):
        h = lax.rem(y + d + 4, 4)
        j = lax.rem(h, 2)

        def total():
            one_copy(j, f).wait_recv()
            return (keep[j, f] + recv1[j, f].astype(jnp.float32)).astype(jnp.bfloat16)

        @pl.when(h == zlo)
        def _():
            do_parts[half, f] = total()
            do_copy(half, f).start()

        @pl.when(h == flip1)
        def _():
            send2[f] = total()
            two_copy(f).start()
            side_copy(f).start()

    def arrange(parts, whole):
        for m in range(16):
            xx, f, b = m // 4, m // 2 % 2, m % 2
            whole[m * shard:(m + 1) * shard, :] = parts[b, f, xx * shard:(xx + 1) * shard, :]

    e = 2 * lax.rem(y, 2) - 1
    dl_copy = pltpu.make_async_remote_copy(
        dl_hbm, dl.at[half], dl_sem.at[0], dl_sem.at[1], device_id=side1, device_id_type=MESH
    )
    dl_arrival = pltpu.make_async_remote_copy(
        dl_hbm, dl.at[1 - half], dl_sem.at[0], dl_sem.at[1], device_id=side1, device_id_type=MESH
    )
    dl_copy.start()
    wait_w(at(zf, 0, 0))
    begin(zf)
    first_near(zf)
    first_far(zf)
    second_near(zf, 0)
    second_near(zf, 1)
    wait_w(at(zg, 0, 0))
    begin(zg)
    for c in loads:
        c.wait()
    q_copy = pltpu.make_async_remote_copy(
        q, q_next, q_send.at[0], q_rsem.at[0], device_id=before, device_id_type=MESH
    )
    log_copy = pltpu.make_async_remote_copy(
        logs, log_next, q_send.at[1], q_rsem.at[1], device_id=before, device_id_type=MESH
    )
    q_copy.start()
    log_copy.start()
    second_near(zf, -1)
    second_near(zf, 2)
    second_far(zf, 0)
    first_near(zg)
    dl_arrival.wait_recv()
    group(zf, 0)
    second_far(zf, 1)
    second_far(zf, -1)
    group(zf, e)
    group(zf, -e)
    first_far(zg)
    second_far(zf, 2)
    group(zf, 2)
    def turn(t, carry):
        c = pl.ds(pl.multiple_of(t * HD, HD), HD)
        ao_t[c, :] = ao[:, c].T
        return carry

    lax.fori_loop(0, width // HD, turn, 0)
    second_near(zg, 0)
    second_near(zg, 1)
    combine(zf, 0)
    combine(zf, e)
    second_near(zg, -1)
    second_far(zg, 0)
    group(zg, 0)
    second_near(zg, 2)
    combine(zf, -e)
    combine(zf, 2)
    second_far(zg, 1)
    second_far(zg, -1)
    group(zg, e)
    group(zg, -e)
    combine(zg, 0)
    combine(zg, e)
    second_far(zg, 2)
    group(zg, 2)
    combine(zg, -e)
    combine(zg, 2)
    for f in range(2):
        two_arrival(f).wait_recv()
    arrange(do_parts, do)

    def delta_copy(t):
        return pltpu.make_async_remote_copy(
            delta.at[t], delta_next.at[t], delta_send.at[t], delta_rsem.at[t],
            device_id=before, device_id_type=MESH,
        )

    def back_copy(t):
        return pltpu.make_async_remote_copy(
            dq_send.at[t], dq_recv.at[t], back_send.at[t], back_rsem.at[t],
            device_id=after, device_id_type=MESH,
        )

    def cols(t, n):
        return pl.ds(pl.multiple_of(t * CHUNK + n * HD, HD), HD)

    def row_delta(t, carry):
        for n in range(heads):
            c = cols(t, n)
            prod = do[c, :].astype(jnp.float32) * ao_t[c, :].astype(jnp.float32)
            row = jnp.sum(prod, axis=0, keepdims=True)
            delta[t, n * 4:(n + 1) * 4, :] = jnp.broadcast_to(row, (4, row.shape[1]))
        delta_copy(t).start()
        return carry

    lax.fori_loop(0, chunks, row_delta, 0)

    rows_i = q.shape[0]
    key_at = lax.broadcasted_iota(jnp.int32, (rows_i, rows_i), 0)
    query_at = lax.broadcasted_iota(jnp.int32, (rows_i, rows_i), 1)

    def head_grads(qh, kh, vh, doh, log_row, delta_row, allowed):
        score = dot(kh, qh, NT) * SCALE - log_row
        probs = jnp.exp(jnp.where(allowed, score, MASKED))
        g_value = dot(probs.astype(jnp.bfloat16), doh, NT)
        g_probs = dot(vh, doh, NN)
        low = (probs * (g_probs - delta_row)).astype(jnp.bfloat16)
        g_key = dot(low, qh, NN) * SCALE
        g_query = dot(low, kh, TN) * SCALE
        return g_query, g_key, g_value

    for t in range(chunks):
        for n in range(heads):
            c = slice(t * CHUNK + n * HD, t * CHUNK + (n + 1) * HD)
            own = slice(n * HD, (n + 1) * HD)
            g = head_grads(
                q[:, c], k[:, c], v[:, c], do[c, :],
                logs[t * heads + n:t * heads + n + 1, :], delta[t, n * 4:n * 4 + 1, :],
                key_at <= query_at,
            )
            dq_acc[t, :, own], dk_acc[t, :, own], dv_acc[t, :, own] = g

    q_copy.wait_recv()
    log_copy.wait_recv()
    limit = jnp.where(seq < 63, rows_i, 0)
    for b in range(2):
        for f in range(2):
            do_copy(b, f).wait_recv()
    arrange(next_parts, do_next)
    for t in range(chunks):
        delta_copy(t).wait_recv()
        for n in range(heads):
            c = slice(t * CHUNK + n * HD, t * CHUNK + (n + 1) * HD)
            own = slice(n * HD, (n + 1) * HD)
            g_query, g_key, g_value = head_grads(
                q_next[:, c], k[:, c], v[:, c], do_next[c, :],
                log_next[t * heads + n:t * heads + n + 1, :], delta_next[t, n * 4:n * 4 + 1, :],
                key_at < limit,
            )
            dq_send[t, :, own] = g_query.astype(jnp.bfloat16)
            dk_ref[:, c] = (dk_acc[t, :, own] + g_key).astype(jnp.bfloat16)
            dv_ref[:, c] = (dv_acc[t, :, own] + g_value).astype(jnp.bfloat16)
        back_copy(t).start()

    def close(t, carry):
        back_copy(t).wait_recv()
        c = pl.ds(pl.multiple_of(t * CHUNK, CHUNK), CHUNK)
        dq_ref[:, c] = (dq_acc[t] + dq_recv[t].astype(jnp.float32)).astype(jnp.bfloat16)
        return carry

    lax.fori_loop(0, chunks, close, 0)

    for c in w_sends:
        c.wait_send()
    z_move(62, far).wait_send()

    @pl.when(jnp.logical_not(home))
    def _():
        z_move(63, cross2).wait_send()

    dl_copy.wait_send()
    q_copy.wait_send()
    log_copy.wait_send()

    for b in range(2):
        two_copy(b).wait_send()
        side_copy(b).wait_send()
        do_copy(half, b).wait_send()
        for f in range(2):
            one_copy(b, f).wait_send()

    def drain(t, carry):
        delta_copy(t).wait_send()
        back_copy(t).wait_send()
        return carry

    lax.fori_loop(0, chunks, drain, 0)


def on_device(query_rows, key_rows, value_rows, attn_out, log_total, d_layer, w_output):
    rows, width = query_rows.shape
    n_heads = log_total.shape[0]
    chunks = width // CHUNK
    seqs = lax.axis_size("seq")
    bf, f32 = jnp.bfloat16, jnp.float32
    full = (rows, width)
    cut = (chunks, rows, CHUNK)
    dma = pltpu.SemaphoreType.DMA
    vm = pltpu.VMEM
    part = 4 * w_output.shape[0]
    turned = (width, rows)
    scratch = [
        vm((w_output.shape[0] * seqs, width), bf),
        vm((2,) + full, bf), vm(full, bf), vm(full, bf), vm(full, bf), vm(full, bf), vm(turned, bf),
        vm((n_heads, rows), f32), vm(full, bf), vm((n_heads, rows), f32),
        vm((2, 2, part, rows), f32), vm((2, 2, part, rows), bf), vm((2, 2, part, rows), bf),
        vm((2, part, rows), bf), vm(turned, bf), vm((2, 2, part, rows), bf),
        vm(turned, bf), vm((2, 2, part, rows), bf),
        vm((chunks, 8, rows), f32), vm((chunks, 8, rows), f32),
        vm(cut, f32), vm(cut, f32), vm(cut, f32), vm(cut, bf), vm(cut, bf),
        dma((6,)), dma((64,)), dma((64,)), dma((2,)), dma((2, 2)), dma((2, 2)),
        dma((2,)), dma((2,)), dma((2,)), dma((2,)), dma((2,)),
        dma((2,)), dma((2, 2)), dma((chunks,)), dma((chunks,)),
        dma((chunks,)), dma((chunks,)),
    ]
    out = jax.ShapeDtypeStruct(full, bf)
    return pl.pallas_call(
        kernel,
        out_shape=(out, out, out),
        in_specs=[pl.BlockSpec(memory_space=pl.ANY)] * 7,
        out_specs=[pl.BlockSpec(memory_space=pltpu.VMEM)] * 3,
        scratch_shapes=scratch,
        compiler_params=pltpu.CompilerParams(
            collective_id=0, has_side_effects=True, vmem_limit_bytes=56 * 2**20
        ),
    )(query_rows, key_rows, value_rows, attn_out, log_total, d_layer, w_output)


def solution(mesh):
    spec = P("seq", "head")
    return jax.shard_map(
        on_device,
        mesh=mesh,
        in_specs=(spec, spec, spec, spec, P("head", "seq"), spec, spec),
        out_specs=(spec, spec, spec),
        check_vma=False,
    )
```

```python
import functools

import jax
import jax.numpy as jnp
from jax import lax
from jax.experimental import pallas as pl
from jax.experimental.pallas import tpu as pltpu
from jax.sharding import PartitionSpec as P

HD = 128
SCALE = HD ** (-0.5)
MASKED = -1e30
CHUNK = 256
MESH = pl.DeviceIdType.MESH
NT = (((1,), (1,)), ((), ()))
NN = (((1,), (0,)), ((), ()))
TN = (((0,), (0,)), ((), ()))


def dot(a, b, dims):
    return lax.dot_general(a, b, dims, preferred_element_type=jnp.float32)


def kernel(
    q_hbm, k_hbm, v_hbm, ao_hbm, log_hbm, dl_hbm, w_hbm,
    dq_hbm, dk_hbm, dv_hbm,
    wbuf, dl, q, k, v, ao, ao_t, logs, q_next, log_next,
    keep, send1, recv1, send2, do, do_parts, do_next, next_parts, delta, delta_next,
    dq_acc, dk_acc, dv_acc, dq_send, dq_recv, dq_ref, dk_ref, dv_ref,
    local_sem, w_send, w_recv, dl_sem, one_send, one_recv, two_send, two_recv, side_send,
    q_send, q_rsem, do_send, do_rsem, delta_send, delta_rsem, back_send, back_rsem, out_sem,
):
    seq = lax.axis_index("seq")
    zlo = lax.axis_index("head")
    core = lax.rem(seq, 2)
    zhi = lax.rem(seq // 2, 2)
    x = lax.rem(seq // 4, 4)
    y = seq // 16
    shard = w_hbm.shape[0]
    part = 4 * shard
    width = q.shape[1]
    chunks = width // CHUNK
    heads = CHUNK // HD

    def device(yy, xx, hh, cc):
        return ((lax.rem(yy + 4, 4) * 4 + lax.rem(xx + 4, 4)) * 2 + hh) * 2 + cc

    flip1 = zlo + 1 - 2 * lax.rem(zlo, 2)
    flip2 = lax.rem(zlo + 2, 4)
    sibling = (device(y, x, zhi, 1 - core), zlo)
    far = (device(y, x, 1 - zhi, core), zlo)
    cross1 = (device(y, x, zhi, 1 - core), flip1)
    cross2 = (device(y, x, 1 - zhi, 1 - core), flip1)
    before = (lax.rem(seq + 63, 64), zlo)
    after = (lax.rem(seq + 1, 64), zlo)
    side1 = (seq, flip1)
    side2 = (seq, flip2)
    before1 = (lax.rem(seq + 63, 64), flip1)
    after1 = (lax.rem(seq + 1, 64), flip1)

    pair = zlo // 2
    half = lax.rem(zlo, 2)
    home = core == half

    def slot(yy, c, f, xx):
        return ((lax.rem(yy + 4, 4) * 2 + c) * 2 + f) * 4 + lax.rem(xx + 4, 4)

    def place(i, j):
        return y + core * i + (1 - core) * j, x + (1 - core) * i + core * j

    def at(f, i, j):
        yy, xx = place(i, j)
        return slot(yy, core, f, xx)

    def near(i, j):
        yy, xx = place(i, j)
        return (device(yy, xx, zhi, core), zlo)

    loads = [
        pltpu.make_async_copy(src, dst, local_sem.at[n])
        for n, (src, dst) in enumerate(
            [(dl_hbm, dl.at[half]), (q_hbm, q), (k_hbm, k), (v_hbm, v), (ao_hbm, ao), (log_hbm, logs)]
        )
    ]

    def w_rows(s):
        return wbuf.at[pl.ds(pl.multiple_of(s * shard, 16), shard)]

    own_slot = slot(y, half, zhi, x)

    @pl.when(home)
    def _():
        pltpu.make_async_copy(w_hbm, w_rows(own_slot), w_recv.at[own_slot]).start()

    for c in loads:
        c.start()

    barrier = pltpu.get_barrier_semaphore()
    partners = [sibling, far, cross1, cross2, before, after, before1, after1, side1, side2]
    for d in (1, -1):
        partners += [near(d, 0), near(0, d)]
    partners += [near(2, 0)]
    for p in partners:
        pl.semaphore_signal(barrier, inc=1, device_id=p, device_id_type=MESH)
    pl.semaphore_wait(barrier, len(partners))

    w_sends = []

    def w_copy(s, device, n):
        return pltpu.make_async_remote_copy(
            w_rows(s), w_rows(s), w_send.at[n], w_recv.at[s],
            device_id=device, device_id_type=MESH,
        )

    def send_w(s, device):
        c = w_copy(s, device, len(w_sends))
        c.start()
        w_sends.append(c)

    def wait_w(s):
        w_copy(s, sibling, 0).wait_recv()

    def z_move(n, device):
        return pltpu.make_async_remote_copy(
            w_hbm, w_rows(own_slot), w_send.at[n], w_recv.at[own_slot],
            device_id=device, device_id_type=MESH,
        )

    @pl.when(home)
    def _():
        z_move(62, far).start()

    @pl.when(jnp.logical_not(home))
    def _():
        z_move(62, cross1).start()
        z_move(63, cross2).start()

    zf, zg = zhi, 1 - zhi

    def begin(f):
        s = at(f, 0, 0)
        for d in (1, -1, 2):
            send_w(s, near(d, 0))
        for d in (1, -1):
            send_w(s, near(0, d))
        send_w(s, sibling)

    def spread(f, i):
        s = at(f, i, 0)
        for d in (1, -1):
            send_w(s, near(0, d))
        send_w(s, sibling)

    def first_near(f):
        wait_w(at(f, 1, 0))
        wait_w(at(f, -1, 0))
        spread(f, 1)
        spread(f, -1)

    def first_far(f):
        wait_w(at(f, 2, 0))
        spread(f, 2)

    def second_near(f, i):
        for d in (1, -1):
            wait_w(at(f, i, d))
        d = 1 if i in (0, 1) else -1
        send_w(at(f, i, -d), near(0, d))
        for d in (1, -1):
            send_w(at(f, i, d), sibling)

    def second_far(f, i):
        wait_w(at(f, i, 2))
        send_w(at(f, i, 2), sibling)

    def one_copy(j, f):
        return pltpu.make_async_remote_copy(
            send1.at[j, f], recv1.at[j, f], one_send.at[j, f], one_recv.at[j, f],
            device_id=side2, device_id_type=MESH,
        )

    def two_copy(f):
        return pltpu.make_async_remote_copy(
            send2.at[f], do_parts.at[half, f], two_send.at[f], two_recv.at[f],
            device_id=side1, device_id_type=MESH,
        )

    def two_arrival(f):
        return pltpu.make_async_remote_copy(
            send2.at[f], do_parts.at[1 - half, f], two_send.at[f], two_recv.at[f],
            device_id=side1, device_id_type=MESH,
        )

    def do_copy(b, f):
        return pltpu.make_async_remote_copy(
            do_parts.at[b, f], next_parts.at[b, f], do_send.at[f], do_rsem.at[b, f],
            device_id=before, device_id_type=MESH,
        )

    def side_copy(f):
        return pltpu.make_async_remote_copy(
            send2.at[f], next_parts.at[half, f], side_send.at[f], do_rsem.at[half, f],
            device_id=before1, device_id_type=MESH,
        )

    def group(f, d):
        h = lax.rem(y + d + 4, 4)
        for xx in range(4):
            wait_w(slot(h, 1 - core, f, xx))
        mine = h // 2 == pair
        j = lax.rem(h, 2)

        def product():
            total = 0.0
            for c in range(2):
                rows = pl.ds(pl.multiple_of(slot(h, c, f, 0) * shard, 16), part)
                total += dot(wbuf[rows, :], dl[c], NT)
            return total

        @pl.when(mine)
        def _():
            keep[j, f] = product()

        @pl.when(jnp.logical_not(mine))
        def _():
            send1[j, f] = product().astype(jnp.bfloat16)
            one_copy(j, f).start()

    def combine(f, d):
        h = lax.rem(y + d + 4, 4)
        j = lax.rem(h, 2)

        def total():
            one_copy(j, f).wait_recv()
            return (keep[j, f] + recv1[j, f].astype(jnp.float32)).astype(jnp.bfloat16)

        @pl.when(h == zlo)
        def _():
            do_parts[half, f] = total()
            do_copy(half, f).start()

        @pl.when(h == flip1)
        def _():
            send2[f] = total()
            two_copy(f).start()
            side_copy(f).start()

    def arrange(parts, whole):
        for m in range(16):
            xx, f, b = m // 4, m // 2 % 2, m % 2
            whole[m * shard:(m + 1) * shard, :] = parts[b, f, xx * shard:(xx + 1) * shard, :]

    e = 2 * lax.rem(y, 2) - 1
    dl_copy = pltpu.make_async_remote_copy(
        dl_hbm, dl.at[half], dl_sem.at[0], dl_sem.at[1], device_id=side1, device_id_type=MESH
    )
    dl_arrival = pltpu.make_async_remote_copy(
        dl_hbm, dl.at[1 - half], dl_sem.at[0], dl_sem.at[1], device_id=side1, device_id_type=MESH
    )
    dl_copy.start()
    wait_w(at(zf, 0, 0))
    begin(zf)
    first_near(zf)
    first_far(zf)
    second_near(zf, 0)
    second_near(zf, 1)
    wait_w(at(zg, 0, 0))
    begin(zg)
    for c in loads:
        c.wait()
    q_copy = pltpu.make_async_remote_copy(
        q, q_next, q_send.at[0], q_rsem.at[0], device_id=before, device_id_type=MESH
    )
    log_copy = pltpu.make_async_remote_copy(
        logs, log_next, q_send.at[1], q_rsem.at[1], device_id=before, device_id_type=MESH
    )
    q_copy.start()
    log_copy.start()
    second_near(zf, -1)
    second_near(zf, 2)
    second_far(zf, 0)
    first_near(zg)
    dl_arrival.wait_recv()
    group(zf, 0)
    second_far(zf, 1)
    second_far(zf, -1)
    group(zf, e)
    group(zf, -e)
    first_far(zg)
    second_far(zf, 2)
    group(zf, 2)
    def turn(t, carry):
        c = pl.ds(pl.multiple_of(t * HD, HD), HD)
        ao_t[c, :] = ao[:, c].T
        return carry

    lax.fori_loop(0, width // HD, turn, 0)
    second_near(zg, 0)
    second_near(zg, 1)
    combine(zf, 0)
    combine(zf, e)
    second_near(zg, -1)
    second_far(zg, 0)
    group(zg, 0)
    second_near(zg, 2)
    combine(zf, -e)
    combine(zf, 2)
    second_far(zg, 1)
    second_far(zg, -1)
    group(zg, e)
    group(zg, -e)
    combine(zg, 0)
    combine(zg, e)
    second_far(zg, 2)
    group(zg, 2)
    combine(zg, -e)
    combine(zg, 2)
    for f in range(2):
        two_arrival(f).wait_recv()
    arrange(do_parts, do)

    def delta_copy(t):
        return pltpu.make_async_remote_copy(
            delta.at[t], delta_next.at[t], delta_send.at[t], delta_rsem.at[t],
            device_id=before, device_id_type=MESH,
        )

    def back_copy(t):
        return pltpu.make_async_remote_copy(
            dq_send.at[t], dq_recv.at[t], back_send.at[t], back_rsem.at[t],
            device_id=after, device_id_type=MESH,
        )

    def out_copy(n, t):
        src, dst = ((dq_ref, dq_hbm), (dk_ref, dk_hbm), (dv_ref, dv_hbm))[n]
        c = pl.ds(t * CHUNK, CHUNK)
        return pltpu.make_async_copy(src.at[:, c], dst.at[:, c], out_sem.at[n, t])

    def cols(t, n):
        return pl.ds(pl.multiple_of(t * CHUNK + n * HD, HD), HD)

    def row_delta(t, carry):
        for n in range(heads):
            c = cols(t, n)
            prod = do[c, :].astype(jnp.float32) * ao_t[c, :].astype(jnp.float32)
            row = jnp.sum(prod, axis=0, keepdims=True)
            delta[t, n * 4:(n + 1) * 4, :] = jnp.broadcast_to(row, (4, row.shape[1]))
        delta_copy(t).start()
        return carry

    lax.fori_loop(0, chunks, row_delta, 0)

    rows_i = q.shape[0]
    key_at = lax.broadcasted_iota(jnp.int32, (rows_i, rows_i), 0)
    query_at = lax.broadcasted_iota(jnp.int32, (rows_i, rows_i), 1)

    def head_grads(qh, kh, vh, doh, log_row, delta_row, allowed):
        score = dot(kh, qh, NT) * SCALE - log_row
        probs = jnp.exp(jnp.where(allowed, score, MASKED))
        g_value = dot(probs.astype(jnp.bfloat16), doh, NT)
        g_probs = dot(vh, doh, NN)
        low = (probs * (g_probs - delta_row)).astype(jnp.bfloat16)
        g_key = dot(low, qh, NN) * SCALE
        g_query = dot(low, kh, TN) * SCALE
        return g_query, g_key, g_value

    for t in range(chunks):
        for n in range(heads):
            c = slice(t * CHUNK + n * HD, t * CHUNK + (n + 1) * HD)
            own = slice(n * HD, (n + 1) * HD)
            g = head_grads(
                q[:, c], k[:, c], v[:, c], do[c, :],
                logs[t * heads + n:t * heads + n + 1, :], delta[t, n * 4:n * 4 + 1, :],
                key_at <= query_at,
            )
            dq_acc[t, :, own], dk_acc[t, :, own], dv_acc[t, :, own] = g

    q_copy.wait_recv()
    log_copy.wait_recv()
    limit = jnp.where(seq < 63, rows_i, 0)
    for b in range(2):
        for f in range(2):
            do_copy(b, f).wait_recv()
    arrange(next_parts, do_next)
    for t in range(chunks):
        delta_copy(t).wait_recv()
        for n in range(heads):
            c = slice(t * CHUNK + n * HD, t * CHUNK + (n + 1) * HD)
            own = slice(n * HD, (n + 1) * HD)
            g_query, g_key, g_value = head_grads(
                q_next[:, c], k[:, c], v[:, c], do_next[c, :],
                log_next[t * heads + n:t * heads + n + 1, :], delta_next[t, n * 4:n * 4 + 1, :],
                key_at < limit,
            )
            dq_send[t, :, own] = g_query.astype(jnp.bfloat16)
            dk_ref[:, c] = (dk_acc[t, :, own] + g_key).astype(jnp.bfloat16)
            dv_ref[:, c] = (dv_acc[t, :, own] + g_value).astype(jnp.bfloat16)
        back_copy(t).start()
        out_copy(1, t).start()
        out_copy(2, t).start()

    for c in w_sends:
        c.wait_send()
    for t in range(chunks):
        back_copy(t).wait_recv()
        c = slice(t * CHUNK, (t + 1) * CHUNK)
        dq_ref[:, c] = (dq_acc[t] + dq_recv[t].astype(jnp.float32)).astype(jnp.bfloat16)
        out_copy(0, t).start()

    z_move(62, far).wait_send()

    @pl.when(jnp.logical_not(home))
    def _():
        z_move(63, cross2).wait_send()

    dl_copy.wait_send()
    q_copy.wait_send()
    log_copy.wait_send()

    for b in range(2):
        two_copy(b).wait_send()
        side_copy(b).wait_send()
        do_copy(half, b).wait_send()
        for f in range(2):
            one_copy(b, f).wait_send()

    def drain(t, carry):
        delta_copy(t).wait_send()
        back_copy(t).wait_send()
        return carry

    lax.fori_loop(0, chunks, drain, 0)
    for n in range(3):
        for t in range(chunks):
            out_copy(n, t).wait()


def hand_over(a, b, c, x, y, z, hold, sem):
    pairs = [(a, x), (b, y), (c, z)]
    arrive = [pltpu.make_async_copy(src, hold.at[n], sem.at[0, n]) for n, (src, dst) in enumerate(pairs)]
    leave = [pltpu.make_async_copy(hold.at[n], dst, sem.at[1, n]) for n, (src, dst) in enumerate(pairs)]
    for copy in arrive:
        copy.start()
    for n in range(3):
        arrive[n].wait()
        leave[n].start()
    for copy in leave:
        copy.wait()


def on_device(query_rows, key_rows, value_rows, attn_out, log_total, d_layer, w_output):
    rows, width = query_rows.shape
    n_heads = log_total.shape[0]
    chunks = width // CHUNK
    seqs = lax.axis_size("seq")
    bf, f32 = jnp.bfloat16, jnp.float32
    full = (rows, width)
    cut = (chunks, rows, CHUNK)
    dma = pltpu.SemaphoreType.DMA
    vm = pltpu.VMEM
    part = 4 * w_output.shape[0]
    turned = (width, rows)
    scratch = [
        vm((w_output.shape[0] * seqs, width), bf),
        vm((2,) + full, bf), vm(full, bf), vm(full, bf), vm(full, bf), vm(full, bf), vm(turned, bf),
        vm((n_heads, rows), f32), vm(full, bf), vm((n_heads, rows), f32),
        vm((2, 2, part, rows), f32), vm((2, 2, part, rows), bf), vm((2, 2, part, rows), bf),
        vm((2, part, rows), bf), vm(turned, bf), vm((2, 2, part, rows), bf),
        vm(turned, bf), vm((2, 2, part, rows), bf),
        vm((chunks, 8, rows), f32), vm((chunks, 8, rows), f32),
        vm(cut, f32), vm(cut, f32), vm(cut, f32), vm(cut, bf), vm(cut, bf),
        vm(full, bf), vm(full, bf), vm(full, bf),
        dma((6,)), dma((64,)), dma((64,)), dma((2,)), dma((2, 2)), dma((2, 2)),
        dma((2,)), dma((2,)), dma((2,)), dma((2,)), dma((2,)),
        dma((2,)), dma((2, 2)), dma((chunks,)), dma((chunks,)),
        dma((chunks,)), dma((chunks,)), dma((3, chunks)),
    ]
    out = jax.ShapeDtypeStruct(full, bf)
    grads = pl.pallas_call(
        kernel,
        out_shape=(out, out, out),
        in_specs=[pl.BlockSpec(memory_space=pl.ANY)] * 7,
        out_specs=[pl.BlockSpec(memory_space=pl.ANY)] * 3,
        scratch_shapes=scratch,
        compiler_params=pltpu.CompilerParams(
            collective_id=0, has_side_effects=True, vmem_limit_bytes=56 * 2**20
        ),
    )(query_rows, key_rows, value_rows, attn_out, log_total, d_layer, w_output)
    return pl.pallas_call(
        hand_over,
        out_shape=(out, out, out),
        in_specs=[pl.BlockSpec(memory_space=pl.ANY)] * 3,
        out_specs=[pl.BlockSpec(memory_space=pl.ANY)] * 3,
        scratch_shapes=[vm((3,) + full, bf), dma((2, 3))],
    )(*grads)


def solution(mesh):
    spec = P("seq", "head")
    return jax.shard_map(
        on_device,
        mesh=mesh,
        in_specs=(spec, spec, spec, spec, P("head", "seq"), spec, spec),
        out_specs=(spec, spec, spec),
        check_vma=False,
    )
```

```python
import functools

import jax
import jax.numpy as jnp
from jax import lax
from jax.experimental import pallas as pl
from jax.experimental.pallas import tpu as pltpu
from jax.sharding import PartitionSpec as P

HD = 128
SCALE = HD ** (-0.5)
MASKED = -1e30
CHUNK = 256
MESH = pl.DeviceIdType.MESH
NT = (((1,), (1,)), ((), ()))
NN = (((1,), (0,)), ((), ()))
TN = (((0,), (0,)), ((), ()))


def dot(a, b, dims):
    return lax.dot_general(a, b, dims, preferred_element_type=jnp.float32)


def kernel(
    q_hbm, k_hbm, v_hbm, ao_hbm, log_hbm, dl_hbm, w_hbm,
    dq_hbm, dk_hbm, dv_hbm,
    wbuf, dl, q, k, v, ao, ao_t, logs, q_next, log_next,
    keep, send1, recv1, send2, do, do_parts, do_next, next_parts, delta, delta_next,
    dq_acc, dk_acc, dv_acc, dq_send, dq_recv, dq_ref, dk_ref, dv_ref,
    local_sem, w_send, w_recv, dl_sem, one_send, one_recv, two_send, two_recv, side_send,
    q_send, q_rsem, do_send, do_rsem, delta_send, delta_rsem, back_send, back_rsem, out_sem,
):
    seq = lax.axis_index("seq")
    zlo = lax.axis_index("head")
    core = lax.rem(seq, 2)
    zhi = lax.rem(seq // 2, 2)
    x = lax.rem(seq // 4, 4)
    y = seq // 16
    shard = w_hbm.shape[0]
    part = 4 * shard
    width = q.shape[1]
    chunks = width // CHUNK
    heads = CHUNK // HD

    def device(yy, xx, hh, cc):
        return ((lax.rem(yy + 4, 4) * 4 + lax.rem(xx + 4, 4)) * 2 + hh) * 2 + cc

    flip1 = zlo + 1 - 2 * lax.rem(zlo, 2)
    flip2 = lax.rem(zlo + 2, 4)
    sibling = (device(y, x, zhi, 1 - core), zlo)
    far = (device(y, x, 1 - zhi, core), zlo)
    cross1 = (device(y, x, zhi, 1 - core), flip1)
    cross2 = (device(y, x, 1 - zhi, 1 - core), flip1)
    before = (lax.rem(seq + 63, 64), zlo)
    after = (lax.rem(seq + 1, 64), zlo)
    side1 = (seq, flip1)
    side2 = (seq, flip2)
    before1 = (lax.rem(seq + 63, 64), flip1)
    after1 = (lax.rem(seq + 1, 64), flip1)

    pair = zlo // 2
    half = lax.rem(zlo, 2)
    home = core == half

    def slot(yy, c, f, xx):
        return ((lax.rem(yy + 4, 4) * 2 + c) * 2 + f) * 4 + lax.rem(xx + 4, 4)

    def place(i, j):
        return y + core * i + (1 - core) * j, x + (1 - core) * i + core * j

    def at(f, i, j):
        yy, xx = place(i, j)
        return slot(yy, core, f, xx)

    def near(i, j):
        yy, xx = place(i, j)
        return (device(yy, xx, zhi, core), zlo)

    loads = [
        pltpu.make_async_copy(src, dst, local_sem.at[n])
        for n, (src, dst) in enumerate(
            [(dl_hbm, dl.at[half]), (q_hbm, q), (k_hbm, k), (v_hbm, v), (ao_hbm, ao), (log_hbm, logs)]
        )
    ]

    def w_rows(s):
        return wbuf.at[pl.ds(pl.multiple_of(s * shard, 16), shard)]

    own_slot = slot(y, half, zhi, x)

    @pl.when(home)
    def _():
        pltpu.make_async_copy(w_hbm, w_rows(own_slot), w_recv.at[own_slot]).start()

    for c in loads:
        c.start()

    barrier = pltpu.get_barrier_semaphore()
    partners = [sibling, far, cross1, cross2, before, after, before1, after1, side1, side2]
    for d in (1, -1):
        partners += [near(d, 0), near(0, d)]
    partners += [near(2, 0)]
    for p in partners:
        pl.semaphore_signal(barrier, inc=1, device_id=p, device_id_type=MESH)
    pl.semaphore_wait(barrier, len(partners))

    w_sends = []

    def w_copy(s, device, n):
        return pltpu.make_async_remote_copy(
            w_rows(s), w_rows(s), w_send.at[n], w_recv.at[s],
            device_id=device, device_id_type=MESH,
        )

    def send_w(s, device):
        c = w_copy(s, device, len(w_sends))
        c.start()
        w_sends.append(c)

    def wait_w(s):
        w_copy(s, sibling, 0).wait_recv()

    def z_move(n, device):
        return pltpu.make_async_remote_copy(
            w_hbm, w_rows(own_slot), w_send.at[n], w_recv.at[own_slot],
            device_id=device, device_id_type=MESH,
        )

    @pl.when(home)
    def _():
        z_move(62, far).start()

    @pl.when(jnp.logical_not(home))
    def _():
        z_move(62, cross1).start()
        z_move(63, cross2).start()

    zf, zg = zhi, 1 - zhi

    def begin(f):
        s = at(f, 0, 0)
        for d in (1, -1, 2):
            send_w(s, near(d, 0))
        for d in (1, -1):
            send_w(s, near(0, d))
        send_w(s, sibling)

    def spread(f, i):
        s = at(f, i, 0)
        for d in (1, -1):
            send_w(s, near(0, d))
        send_w(s, sibling)

    def first_near(f):
        wait_w(at(f, 1, 0))
        wait_w(at(f, -1, 0))
        spread(f, 1)
        spread(f, -1)

    def first_far(f):
        wait_w(at(f, 2, 0))
        spread(f, 2)

    def second_near(f, i):
        for d in (1, -1):
            wait_w(at(f, i, d))
        d = 1 if i in (0, 1) else -1
        send_w(at(f, i, -d), near(0, d))
        for d in (1, -1):
            send_w(at(f, i, d), sibling)

    def second_far(f, i):
        wait_w(at(f, i, 2))
        send_w(at(f, i, 2), sibling)

    def one_copy(j, f):
        return pltpu.make_async_remote_copy(
            send1.at[j, f], recv1.at[j, f], one_send.at[j, f], one_recv.at[j, f],
            device_id=side2, device_id_type=MESH,
        )

    def two_copy(f):
        return pltpu.make_async_remote_copy(
            send2.at[f], do_parts.at[half, f], two_send.at[f], two_recv.at[f],
            device_id=side1, device_id_type=MESH,
        )

    def two_arrival(f):
        return pltpu.make_async_remote_copy(
            send2.at[f], do_parts.at[1 - half, f], two_send.at[f], two_recv.at[f],
            device_id=side1, device_id_type=MESH,
        )

    def do_copy(b, f):
        return pltpu.make_async_remote_copy(
            do_parts.at[b, f], next_parts.at[b, f], do_send.at[f], do_rsem.at[b, f],
            device_id=before, device_id_type=MESH,
        )

    def side_copy(f):
        return pltpu.make_async_remote_copy(
            send2.at[f], next_parts.at[half, f], side_send.at[f], do_rsem.at[half, f],
            device_id=before1, device_id_type=MESH,
        )

    def product(f, h):
        for xx in range(4):
            wait_w(slot(h, 1 - core, f, xx))
        total = 0.0
        for c in range(2):
            rows = pl.ds(pl.multiple_of(slot(h, c, f, 0) * shard, 16), part)
            total += dot(wbuf[rows, :], dl[c], NT)
        return total

    def send_groups(f):
        for h in (3 - zlo, flip2):
            j = lax.rem(h, 2)
            send1[j, f] = product(f, h).astype(jnp.bfloat16)
            one_copy(j, f).start()

    def keep_groups(f):
        for h in (flip1, zlo):
            keep[lax.rem(h, 2), f] = product(f, h)

    def combine(f):
        def total(j):
            one_copy(j, f).wait_recv()
            return (keep[j, f] + recv1[j, f].astype(jnp.float32)).astype(jnp.bfloat16)

        send2[f] = total(1 - half)
        two_copy(f).start()
        side_copy(f).start()
        do_parts[half, f] = total(half)
        do_copy(half, f).start()

    def arrange(parts, whole):
        for m in range(16):
            xx, f, b = m // 4, m // 2 % 2, m % 2
            whole[m * shard:(m + 1) * shard, :] = parts[b, f, xx * shard:(xx + 1) * shard, :]

    dl_copy = pltpu.make_async_remote_copy(
        dl_hbm, dl.at[half], dl_sem.at[0], dl_sem.at[1], device_id=side1, device_id_type=MESH
    )
    dl_arrival = pltpu.make_async_remote_copy(
        dl_hbm, dl.at[1 - half], dl_sem.at[0], dl_sem.at[1], device_id=side1, device_id_type=MESH
    )
    dl_copy.start()
    wait_w(at(zf, 0, 0))
    begin(zf)
    first_near(zf)
    first_far(zf)
    second_near(zf, 0)
    second_near(zf, 1)
    wait_w(at(zg, 0, 0))
    begin(zg)
    for c in loads:
        c.wait()
    q_copy = pltpu.make_async_remote_copy(
        q, q_next, q_send.at[0], q_rsem.at[0], device_id=before, device_id_type=MESH
    )
    log_copy = pltpu.make_async_remote_copy(
        logs, log_next, q_send.at[1], q_rsem.at[1], device_id=before, device_id_type=MESH
    )
    q_copy.start()
    log_copy.start()
    second_near(zf, -1)
    second_near(zf, 2)
    first_near(zg)
    second_far(zf, 0)
    second_far(zf, 1)
    second_far(zf, -1)
    first_far(zg)
    second_far(zf, 2)
    dl_arrival.wait_recv()
    send_groups(zf)
    second_near(zg, 0)
    second_near(zg, 1)
    keep_groups(zf)
    second_near(zg, -1)
    second_near(zg, 2)

    def turn(t, carry):
        c = pl.ds(pl.multiple_of(t * HD, HD), HD)
        ao_t[c, :] = ao[:, c].T
        return carry

    lax.fori_loop(0, width // HD, turn, 0)
    second_far(zg, 0)
    second_far(zg, 1)
    second_far(zg, -1)
    second_far(zg, 2)
    send_groups(zg)
    combine(zf)
    keep_groups(zg)
    combine(zg)
    for f in range(2):
        two_arrival(f).wait_recv()
    arrange(do_parts, do)

    def delta_copy(t):
        return pltpu.make_async_remote_copy(
            delta.at[t], delta_next.at[t], delta_send.at[t], delta_rsem.at[t],
            device_id=before, device_id_type=MESH,
        )

    def back_copy(t):
        return pltpu.make_async_remote_copy(
            dq_send.at[t], dq_recv.at[t], back_send.at[t], back_rsem.at[t],
            device_id=after, device_id_type=MESH,
        )

    def out_copy(n, t):
        src, dst = ((dq_ref, dq_hbm), (dk_ref, dk_hbm), (dv_ref, dv_hbm))[n]
        c = pl.ds(t * CHUNK, CHUNK)
        return pltpu.make_async_copy(src.at[:, c], dst.at[:, c], out_sem.at[n, t])

    def cols(t, n):
        return pl.ds(pl.multiple_of(t * CHUNK + n * HD, HD), HD)

    def row_delta(t, carry):
        for n in range(heads):
            c = cols(t, n)
            prod = do[c, :].astype(jnp.float32) * ao_t[c, :].astype(jnp.float32)
            row = jnp.sum(prod, axis=0, keepdims=True)
            delta[t, n * 4:(n + 1) * 4, :] = jnp.broadcast_to(row, (4, row.shape[1]))
        delta_copy(t).start()
        return carry

    lax.fori_loop(0, chunks, row_delta, 0)

    rows_i = q.shape[0]
    key_at = lax.broadcasted_iota(jnp.int32, (rows_i, rows_i), 0)
    query_at = lax.broadcasted_iota(jnp.int32, (rows_i, rows_i), 1)

    def head_grads(qh, kh, vh, doh, log_row, delta_row, allowed):
        score = dot(kh, qh, NT) * SCALE - log_row
        probs = jnp.exp(jnp.where(allowed, score, MASKED))
        g_value = dot(probs.astype(jnp.bfloat16), doh, NT)
        g_probs = dot(vh, doh, NN)
        low = (probs * (g_probs - delta_row)).astype(jnp.bfloat16)
        g_key = dot(low, qh, NN) * SCALE
        g_query = dot(low, kh, TN) * SCALE
        return g_query, g_key, g_value

    for t in range(chunks):
        for n in range(heads):
            c = slice(t * CHUNK + n * HD, t * CHUNK + (n + 1) * HD)
            own = slice(n * HD, (n + 1) * HD)
            g = head_grads(
                q[:, c], k[:, c], v[:, c], do[c, :],
                logs[t * heads + n:t * heads + n + 1, :], delta[t, n * 4:n * 4 + 1, :],
                key_at <= query_at,
            )
            dq_acc[t, :, own], dk_acc[t, :, own], dv_acc[t, :, own] = g

    q_copy.wait_recv()
    log_copy.wait_recv()
    limit = jnp.where(seq < 63, rows_i, 0)
    for b in range(2):
        for f in range(2):
            do_copy(b, f).wait_recv()
    arrange(next_parts, do_next)
    for t in range(chunks):
        delta_copy(t).wait_recv()
        for n in range(heads):
            c = slice(t * CHUNK + n * HD, t * CHUNK + (n + 1) * HD)
            own = slice(n * HD, (n + 1) * HD)
            g_query, g_key, g_value = head_grads(
                q_next[:, c], k[:, c], v[:, c], do_next[c, :],
                log_next[t * heads + n:t * heads + n + 1, :], delta_next[t, n * 4:n * 4 + 1, :],
                key_at < limit,
            )
            dq_send[t, :, own] = g_query.astype(jnp.bfloat16)
            dk_ref[:, c] = (dk_acc[t, :, own] + g_key).astype(jnp.bfloat16)
            dv_ref[:, c] = (dv_acc[t, :, own] + g_value).astype(jnp.bfloat16)
        back_copy(t).start()
        out_copy(1, t).start()
        out_copy(2, t).start()

    for c in w_sends:
        c.wait_send()
    for t in range(chunks):
        back_copy(t).wait_recv()
        c = slice(t * CHUNK, (t + 1) * CHUNK)
        dq_ref[:, c] = (dq_acc[t] + dq_recv[t].astype(jnp.float32)).astype(jnp.bfloat16)
        out_copy(0, t).start()

    z_move(62, far).wait_send()

    @pl.when(jnp.logical_not(home))
    def _():
        z_move(63, cross2).wait_send()

    dl_copy.wait_send()
    q_copy.wait_send()
    log_copy.wait_send()

    for b in range(2):
        two_copy(b).wait_send()
        side_copy(b).wait_send()
        do_copy(half, b).wait_send()
        for f in range(2):
            one_copy(b, f).wait_send()

    def drain(t, carry):
        delta_copy(t).wait_send()
        back_copy(t).wait_send()
        return carry

    lax.fori_loop(0, chunks, drain, 0)
    for n in range(3):
        for t in range(chunks):
            out_copy(n, t).wait()


def hand_over(a, b, c, x, y, z, hold, sem):
    pairs = [(a, x), (b, y), (c, z)]
    arrive = [pltpu.make_async_copy(src, hold.at[n], sem.at[0, n]) for n, (src, dst) in enumerate(pairs)]
    leave = [pltpu.make_async_copy(hold.at[n], dst, sem.at[1, n]) for n, (src, dst) in enumerate(pairs)]
    for copy in arrive:
        copy.start()
    for n in range(3):
        arrive[n].wait()
        leave[n].start()
    for copy in leave:
        copy.wait()


def on_device(query_rows, key_rows, value_rows, attn_out, log_total, d_layer, w_output):
    rows, width = query_rows.shape
    n_heads = log_total.shape[0]
    chunks = width // CHUNK
    seqs = lax.axis_size("seq")
    bf, f32 = jnp.bfloat16, jnp.float32
    full = (rows, width)
    cut = (chunks, rows, CHUNK)
    dma = pltpu.SemaphoreType.DMA
    vm = pltpu.VMEM
    part = 4 * w_output.shape[0]
    turned = (width, rows)
    scratch = [
        vm((w_output.shape[0] * seqs, width), bf),
        vm((2,) + full, bf), vm(full, bf), vm(full, bf), vm(full, bf), vm(full, bf), vm(turned, bf),
        vm((n_heads, rows), f32), vm(full, bf), vm((n_heads, rows), f32),
        vm((2, 2, part, rows), f32), vm((2, 2, part, rows), bf), vm((2, 2, part, rows), bf),
        vm((2, part, rows), bf), vm(turned, bf), vm((2, 2, part, rows), bf),
        vm(turned, bf), vm((2, 2, part, rows), bf),
        vm((chunks, 8, rows), f32), vm((chunks, 8, rows), f32),
        vm(cut, f32), vm(cut, f32), vm(cut, f32), vm(cut, bf), vm(cut, bf),
        vm(full, bf), vm(full, bf), vm(full, bf),
        dma((6,)), dma((64,)), dma((64,)), dma((2,)), dma((2, 2)), dma((2, 2)),
        dma((2,)), dma((2,)), dma((2,)), dma((2,)), dma((2,)),
        dma((2,)), dma((2, 2)), dma((chunks,)), dma((chunks,)),
        dma((chunks,)), dma((chunks,)), dma((3, chunks)),
    ]
    out = jax.ShapeDtypeStruct(full, bf)
    grads = pl.pallas_call(
        kernel,
        out_shape=(out, out, out),
        in_specs=[pl.BlockSpec(memory_space=pl.ANY)] * 7,
        out_specs=[pl.BlockSpec(memory_space=pl.ANY)] * 3,
        scratch_shapes=scratch,
        compiler_params=pltpu.CompilerParams(
            collective_id=0, has_side_effects=True, vmem_limit_bytes=56 * 2**20
        ),
    )(query_rows, key_rows, value_rows, attn_out, log_total, d_layer, w_output)
    return pl.pallas_call(
        hand_over,
        out_shape=(out, out, out),
        in_specs=[pl.BlockSpec(memory_space=pl.ANY)] * 3,
        out_specs=[pl.BlockSpec(memory_space=pl.ANY)] * 3,
        scratch_shapes=[vm((3,) + full, bf), dma((2, 3))],
    )(*grads)


def solution(mesh):
    spec = P("seq", "head")
    return jax.shard_map(
        on_device,
        mesh=mesh,
        in_specs=(spec, spec, spec, spec, P("head", "seq"), spec, spec),
        out_specs=(spec, spec, spec),
        check_vma=False,
    )
```

```python
import functools

import jax
import jax.numpy as jnp
from jax import lax
from jax.experimental import pallas as pl
from jax.experimental.pallas import tpu as pltpu
from jax.sharding import PartitionSpec as P

HD = 128
SCALE = HD ** (-0.5)
MASKED = -1e30
CHUNK = 256
MESH = pl.DeviceIdType.MESH
NT = (((1,), (1,)), ((), ()))
NN = (((1,), (0,)), ((), ()))
TN = (((0,), (0,)), ((), ()))


def dot(a, b, dims):
    return lax.dot_general(a, b, dims, preferred_element_type=jnp.float32)


def kernel(
    q_hbm, k_hbm, v_hbm, ao_hbm, log_hbm, dl_hbm, w_hbm,
    dq_hbm, dk_hbm, dv_hbm,
    wbuf, dl, q, k, v, ao, ao_t, logs, q_next, log_next,
    keep, send1, recv1, send2, do, do_parts, do_next, next_parts, delta, delta_next,
    dq_acc, dk_acc, dv_acc, dq_send, dq_recv, dq_ref, dk_ref, dv_ref,
    local_sem, w_send, w_recv, dl_sem, one_send, one_recv, two_send, two_recv, side_send,
    q_send, q_rsem, do_send, do_rsem, delta_send, delta_rsem, back_send, back_rsem, out_sem,
):
    seq = lax.axis_index("seq")
    zlo = lax.axis_index("head")
    core = lax.rem(seq, 2)
    zhi = lax.rem(seq // 2, 2)
    x = lax.rem(seq // 4, 4)
    y = seq // 16
    shard = w_hbm.shape[0]
    part = 4 * shard
    width = q.shape[1]
    chunks = width // CHUNK
    heads = CHUNK // HD

    def device(yy, xx, hh, cc):
        return ((lax.rem(yy + 4, 4) * 4 + lax.rem(xx + 4, 4)) * 2 + hh) * 2 + cc

    flip1 = zlo + 1 - 2 * lax.rem(zlo, 2)
    flip2 = lax.rem(zlo + 2, 4)
    sibling = (device(y, x, zhi, 1 - core), zlo)
    far = (device(y, x, 1 - zhi, core), zlo)
    cross1 = (device(y, x, zhi, 1 - core), flip1)
    cross2 = (device(y, x, 1 - zhi, 1 - core), flip1)
    before = (lax.rem(seq + 63, 64), zlo)
    after = (lax.rem(seq + 1, 64), zlo)
    side1 = (seq, flip1)
    side2 = (seq, flip2)
    before1 = (lax.rem(seq + 63, 64), flip1)
    after1 = (lax.rem(seq + 1, 64), flip1)

    pair = zlo // 2
    half = lax.rem(zlo, 2)
    home = core == half

    def slot(yy, c, f, xx):
        return ((lax.rem(yy + 4, 4) * 2 + c) * 2 + f) * 4 + lax.rem(xx + 4, 4)

    def place(i, j):
        return y + core * i + (1 - core) * j, x + (1 - core) * i + core * j

    def at(f, i, j):
        yy, xx = place(i, j)
        return slot(yy, core, f, xx)

    def near(i, j):
        yy, xx = place(i, j)
        return (device(yy, xx, zhi, core), zlo)

    loads = [
        pltpu.make_async_copy(src, dst, local_sem.at[n])
        for n, (src, dst) in enumerate(
            [(dl_hbm, dl.at[half]), (q_hbm, q), (k_hbm, k), (v_hbm, v), (ao_hbm, ao), (log_hbm, logs)]
        )
    ]

    def w_rows(s):
        return wbuf.at[pl.ds(pl.multiple_of(s * shard, 16), shard)]

    own_slot = slot(y, half, zhi, x)

    @pl.when(home)
    def _():
        pltpu.make_async_copy(w_hbm, w_rows(own_slot), w_recv.at[own_slot]).start()

    for c in loads:
        c.start()

    barrier = pltpu.get_barrier_semaphore()
    partners = [sibling, far, cross1, cross2, before, after, before1, after1, side1, side2]
    for d in (1, -1):
        partners += [near(d, 0), near(0, d)]
    partners += [near(2, 0)]
    for p in partners:
        pl.semaphore_signal(barrier, inc=1, device_id=p, device_id_type=MESH)
    pl.semaphore_wait(barrier, len(partners))

    w_sends = []

    def w_copy(s, device, n):
        return pltpu.make_async_remote_copy(
            w_rows(s), w_rows(s), w_send.at[n], w_recv.at[s],
            device_id=device, device_id_type=MESH,
        )

    def send_w(s, device):
        c = w_copy(s, device, len(w_sends))
        c.start()
        w_sends.append(c)

    def wait_w(s):
        w_copy(s, sibling, 0).wait_recv()

    def z_move(n, device):
        return pltpu.make_async_remote_copy(
            w_hbm, w_rows(own_slot), w_send.at[n], w_recv.at[own_slot],
            device_id=device, device_id_type=MESH,
        )

    @pl.when(home)
    def _():
        z_move(62, far).start()

    @pl.when(jnp.logical_not(home))
    def _():
        z_move(62, cross1).start()
        z_move(63, cross2).start()

    zf, zg = zhi, 1 - zhi

    def begin(f):
        s = at(f, 0, 0)
        for d in (1, -1, 2):
            send_w(s, near(d, 0))
        for d in (1, -1):
            send_w(s, near(0, d))
        send_w(s, sibling)

    def spread(f, i):
        s = at(f, i, 0)
        for d in (1, -1):
            send_w(s, near(0, d))
        send_w(s, sibling)

    def first_near(f):
        wait_w(at(f, 1, 0))
        wait_w(at(f, -1, 0))
        spread(f, 1)
        spread(f, -1)

    def first_far(f):
        wait_w(at(f, 2, 0))
        spread(f, 2)

    def second_near(f, i):
        for d in (1, -1):
            wait_w(at(f, i, d))
        d = 1 if i in (0, 1) else -1
        send_w(at(f, i, -d), near(0, d))
        for d in (1, -1):
            send_w(at(f, i, d), sibling)

    def second_far(f, i):
        wait_w(at(f, i, 2))
        send_w(at(f, i, 2), sibling)

    def one_copy(j, f):
        return pltpu.make_async_remote_copy(
            send1.at[j, f], recv1.at[j, f], one_send.at[j, f], one_recv.at[j, f],
            device_id=side2, device_id_type=MESH,
        )

    def two_copy(f):
        return pltpu.make_async_remote_copy(
            send2.at[f], do_parts.at[half, f], two_send.at[f], two_recv.at[f],
            device_id=side1, device_id_type=MESH,
        )

    def two_arrival(f):
        return pltpu.make_async_remote_copy(
            send2.at[f], do_parts.at[1 - half, f], two_send.at[f], two_recv.at[f],
            device_id=side1, device_id_type=MESH,
        )

    def do_copy(b, f):
        return pltpu.make_async_remote_copy(
            do_parts.at[b, f], next_parts.at[b, f], do_send.at[f], do_rsem.at[b, f],
            device_id=before, device_id_type=MESH,
        )

    def side_copy(f):
        return pltpu.make_async_remote_copy(
            send2.at[f], next_parts.at[half, f], side_send.at[f], do_rsem.at[half, f],
            device_id=before1, device_id_type=MESH,
        )

    def product(f, h):
        for xx in range(4):
            wait_w(slot(h, 1 - core, f, xx))
        total = 0.0
        for c in range(2):
            rows = pl.ds(pl.multiple_of(slot(h, c, f, 0) * shard, 16), part)
            total += dot(wbuf[rows, :], dl[c], NT)
        return total

    def send_groups(f):
        for h in (flip2, 3 - zlo):
            j = lax.rem(h, 2)
            send1[j, f] = product(f, h).astype(jnp.bfloat16)
            one_copy(j, f).start()

    def keep_groups(f):
        for h in (flip1, zlo):
            keep[lax.rem(h, 2), f] = product(f, h)

    def combine(f):
        def total(j):
            one_copy(j, f).wait_recv()
            return (keep[j, f] + recv1[j, f].astype(jnp.float32)).astype(jnp.bfloat16)

        send2[f] = total(1 - half)
        two_copy(f).start()
        side_copy(f).start()
        do_parts[half, f] = total(half)
        do_copy(half, f).start()

    def arrange(parts, whole):
        for m in range(16):
            xx, f, b = m // 4, m // 2 % 2, m % 2
            whole[m * shard:(m + 1) * shard, :] = parts[b, f, xx * shard:(xx + 1) * shard, :]

    dl_copy = pltpu.make_async_remote_copy(
        dl_hbm, dl.at[half], dl_sem.at[0], dl_sem.at[1], device_id=side1, device_id_type=MESH
    )
    dl_arrival = pltpu.make_async_remote_copy(
        dl_hbm, dl.at[1 - half], dl_sem.at[0], dl_sem.at[1], device_id=side1, device_id_type=MESH
    )
    dl_copy.start()
    wait_w(at(zf, 0, 0))
    begin(zf)
    first_near(zf)
    first_far(zf)
    for c in loads:
        c.wait()
    q_copy = pltpu.make_async_remote_copy(
        q, q_next, q_send.at[0], q_rsem.at[0], device_id=before, device_id_type=MESH
    )
    log_copy = pltpu.make_async_remote_copy(
        logs, log_next, q_send.at[1], q_rsem.at[1], device_id=before, device_id_type=MESH
    )
    q_copy.start()
    log_copy.start()
    second_near(zf, 0)
    second_near(zf, 1)
    wait_w(at(zg, 0, 0))
    begin(zg)
    second_near(zf, -1)
    second_near(zf, 2)
    first_near(zg)
    second_far(zf, 0)
    second_far(zf, 1)
    second_far(zf, -1)
    first_far(zg)
    second_far(zf, 2)
    dl_arrival.wait_recv()
    send_groups(zf)
    second_near(zg, 0)
    second_near(zg, 1)
    keep_groups(zf)
    second_near(zg, -1)
    second_near(zg, 2)

    def turn(t, carry):
        c = pl.ds(pl.multiple_of(t * HD, HD), HD)
        ao_t[c, :] = ao[:, c].T
        return carry

    lax.fori_loop(0, width // HD, turn, 0)
    second_far(zg, 0)
    second_far(zg, 1)
    second_far(zg, -1)
    second_far(zg, 2)
    send_groups(zg)
    combine(zf)
    keep_groups(zg)
    combine(zg)
    for f in range(2):
        two_arrival(f).wait_recv()
    arrange(do_parts, do)

    def delta_copy(t):
        return pltpu.make_async_remote_copy(
            delta.at[t], delta_next.at[t], delta_send.at[t], delta_rsem.at[t],
            device_id=before, device_id_type=MESH,
        )

    def back_copy(t):
        return pltpu.make_async_remote_copy(
            dq_send.at[t], dq_recv.at[t], back_send.at[t], back_rsem.at[t],
            device_id=after, device_id_type=MESH,
        )

    def out_copy(n, t):
        src, dst = ((dq_ref, dq_hbm), (dk_ref, dk_hbm), (dv_ref, dv_hbm))[n]
        c = pl.ds(t * CHUNK, CHUNK)
        return pltpu.make_async_copy(src.at[:, c], dst.at[:, c], out_sem.at[n, t])

    def cols(t, n):
        return pl.ds(pl.multiple_of(t * CHUNK + n * HD, HD), HD)

    def row_delta(t, carry):
        for n in range(heads):
            c = cols(t, n)
            prod = do[c, :].astype(jnp.float32) * ao_t[c, :].astype(jnp.float32)
            row = jnp.sum(prod, axis=0, keepdims=True)
            delta[t, n * 4:(n + 1) * 4, :] = jnp.broadcast_to(row, (4, row.shape[1]))
        delta_copy(t).start()
        return carry

    lax.fori_loop(0, chunks, row_delta, 0)

    rows_i = q.shape[0]
    key_at = lax.broadcasted_iota(jnp.int32, (rows_i, rows_i), 0)
    query_at = lax.broadcasted_iota(jnp.int32, (rows_i, rows_i), 1)

    def head_grads(qh, kh, vh, doh, log_row, delta_row, allowed):
        score = dot(kh, qh, NT) * SCALE - log_row
        probs = jnp.exp(jnp.where(allowed, score, MASKED))
        g_value = dot(probs.astype(jnp.bfloat16), doh, NT)
        g_probs = dot(vh, doh, NN)
        low = (probs * (g_probs - delta_row)).astype(jnp.bfloat16)
        g_key = dot(low, qh, NN) * SCALE
        g_query = dot(low, kh, TN) * SCALE
        return g_query, g_key, g_value

    for t in range(chunks):
        for n in range(heads):
            c = slice(t * CHUNK + n * HD, t * CHUNK + (n + 1) * HD)
            own = slice(n * HD, (n + 1) * HD)
            g = head_grads(
                q[:, c], k[:, c], v[:, c], do[c, :],
                logs[t * heads + n:t * heads + n + 1, :], delta[t, n * 4:n * 4 + 1, :],
                key_at <= query_at,
            )
            dq_acc[t, :, own], dk_acc[t, :, own], dv_acc[t, :, own] = g

    q_copy.wait_recv()
    log_copy.wait_recv()
    limit = jnp.where(seq < 63, rows_i, 0)
    for b in range(2):
        for f in range(2):
            do_copy(b, f).wait_recv()
    arrange(next_parts, do_next)
    for t in range(chunks):
        delta_copy(t).wait_recv()
        for n in range(heads):
            c = slice(t * CHUNK + n * HD, t * CHUNK + (n + 1) * HD)
            own = slice(n * HD, (n + 1) * HD)
            g_query, g_key, g_value = head_grads(
                q_next[:, c], k[:, c], v[:, c], do_next[c, :],
                log_next[t * heads + n:t * heads + n + 1, :], delta_next[t, n * 4:n * 4 + 1, :],
                key_at < limit,
            )
            dq_send[t, :, own] = g_query.astype(jnp.bfloat16)
            dk_ref[:, c] = (dk_acc[t, :, own] + g_key).astype(jnp.bfloat16)
            dv_ref[:, c] = (dv_acc[t, :, own] + g_value).astype(jnp.bfloat16)
        back_copy(t).start()
        out_copy(1, t).start()
        out_copy(2, t).start()

    for c in w_sends:
        c.wait_send()
    for t in range(chunks):
        back_copy(t).wait_recv()
        c = slice(t * CHUNK, (t + 1) * CHUNK)
        dq_ref[:, c] = (dq_acc[t] + dq_recv[t].astype(jnp.float32)).astype(jnp.bfloat16)
        out_copy(0, t).start()

    z_move(62, far).wait_send()

    @pl.when(jnp.logical_not(home))
    def _():
        z_move(63, cross2).wait_send()

    dl_copy.wait_send()
    q_copy.wait_send()
    log_copy.wait_send()

    for b in range(2):
        two_copy(b).wait_send()
        side_copy(b).wait_send()
        do_copy(half, b).wait_send()
        for f in range(2):
            one_copy(b, f).wait_send()

    def drain(t, carry):
        delta_copy(t).wait_send()
        back_copy(t).wait_send()
        return carry

    lax.fori_loop(0, chunks, drain, 0)
    for n in range(3):
        for t in range(chunks):
            out_copy(n, t).wait()


def hand_over(a, b, c, x, y, z, hold, sem):
    pairs = [(a, x), (b, y), (c, z)]
    arrive = [pltpu.make_async_copy(src, hold.at[n], sem.at[0, n]) for n, (src, dst) in enumerate(pairs)]
    leave = [pltpu.make_async_copy(hold.at[n], dst, sem.at[1, n]) for n, (src, dst) in enumerate(pairs)]
    for copy in arrive:
        copy.start()
    for n in range(3):
        arrive[n].wait()
        leave[n].start()
    for copy in leave:
        copy.wait()


def on_device(query_rows, key_rows, value_rows, attn_out, log_total, d_layer, w_output):
    rows, width = query_rows.shape
    n_heads = log_total.shape[0]
    chunks = width // CHUNK
    seqs = lax.axis_size("seq")
    bf, f32 = jnp.bfloat16, jnp.float32
    full = (rows, width)
    cut = (chunks, rows, CHUNK)
    dma = pltpu.SemaphoreType.DMA
    vm = pltpu.VMEM
    part = 4 * w_output.shape[0]
    turned = (width, rows)
    scratch = [
        vm((w_output.shape[0] * seqs, width), bf),
        vm((2,) + full, bf), vm(full, bf), vm(full, bf), vm(full, bf), vm(full, bf), vm(turned, bf),
        vm((n_heads, rows), f32), vm(full, bf), vm((n_heads, rows), f32),
        vm((2, 2, part, rows), f32), vm((2, 2, part, rows), bf), vm((2, 2, part, rows), bf),
        vm((2, part, rows), bf), vm(turned, bf), vm((2, 2, part, rows), bf),
        vm(turned, bf), vm((2, 2, part, rows), bf),
        vm((chunks, 8, rows), f32), vm((chunks, 8, rows), f32),
        vm(cut, f32), vm(cut, f32), vm(cut, f32), vm(cut, bf), vm(cut, bf),
        vm(full, bf), vm(full, bf), vm(full, bf),
        dma((6,)), dma((64,)), dma((64,)), dma((2,)), dma((2, 2)), dma((2, 2)),
        dma((2,)), dma((2,)), dma((2,)), dma((2,)), dma((2,)),
        dma((2,)), dma((2, 2)), dma((chunks,)), dma((chunks,)),
        dma((chunks,)), dma((chunks,)), dma((3, chunks)),
    ]
    out = jax.ShapeDtypeStruct(full, bf)
    grads = pl.pallas_call(
        kernel,
        out_shape=(out, out, out),
        in_specs=[pl.BlockSpec(memory_space=pl.ANY)] * 7,
        out_specs=[pl.BlockSpec(memory_space=pl.ANY)] * 3,
        scratch_shapes=scratch,
        compiler_params=pltpu.CompilerParams(
            collective_id=0, has_side_effects=True, vmem_limit_bytes=56 * 2**20
        ),
    )(query_rows, key_rows, value_rows, attn_out, log_total, d_layer, w_output)
    return pl.pallas_call(
        hand_over,
        out_shape=(out, out, out),
        in_specs=[pl.BlockSpec(memory_space=pl.ANY)] * 3,
        out_specs=[pl.BlockSpec(memory_space=pl.ANY)] * 3,
        scratch_shapes=[vm((3,) + full, bf), dma((2, 3))],
    )(*grads)


def solution(mesh):
    spec = P("seq", "head")
    return jax.shard_map(
        on_device,
        mesh=mesh,
        in_specs=(spec, spec, spec, spec, P("head", "seq"), spec, spec),
        out_specs=(spec, spec, spec),
        check_vma=False,
    )
```
